32 devices in a mesh: frame: 8 (over y, x, core), tile: 4 (over z).
Axes of the slice: x: 2, y: 2, z: 4, core: 2. Of those that a mesh axis runs over, the one named last changes fastest.
Arguments:
- grid: bfloat16 [64, 16, 32, 1024], P(None, 'frame', None, 'tile'), may hold values from -6 to 6
- conv_weight: bfloat16 [9, 64, 8], replicated, may hold values from -0.75 to 0.75
- conv_bias: float32 [64], replicated, may hold values from -3 to 3
- depth_kernel: float32 [4, 3, 64], replicated, may hold values from -3 to 3
- point_weight: bfloat16 [4, 64, 64], replicated, may hold values from -0.75 to 0.75
- occupied: int32 [4, 32], P('tile'), may hold values from 0 to 63, as said below
- counts: int32 [4], P('tile'), may hold values from 10 to 32, as said below
Outputs:
- features: bfloat16 [64, 16, 32, 1024], P(None, 'frame', None, 'tile')
The draws below stay inside these ranges and needn't reach their ends.
Inputs may be any that keep to these rules, and one draw needn't show every extreme that they name: Each row holds 32 distinct block numbers of its tile; its first counts[t] entries are the occupied blocks, the rest are unoccupied blocks used as padding. `counts`: some tile's list is fully occupied, and some tile has exactly the fewest occupied entries.
All inputs are finite; a program needn't handle non-finite values.
Results may differ from the reference program's by a relative error of at most 0.0051.
Values may be sent and summed in bfloat16 or wider, within the bound.
No kernel may reach another device: no remote copies, remote signals or barrier semaphores. Data moves between devices by JAX's collectives and lax.ppermute only.
A program may use at most 128 MiB of HBM per device.

```python
import jax
import jax.numpy as jnp
from jax import lax

C = 64
GROUP = 8
LAYERS = 4
ROWS = 32
WDEV = 256
FRAMES = 16
WIDTH = 1024
K_SLOTS = 32
N_TILE = 4


def swapped(values, first, second):
    positions = jnp.arange(values.shape[0], dtype=jnp.int32)
    first_value = values[first]
    second_value = values[second]
    return jnp.where(positions == first, second_value, jnp.where(positions == second, first_value, values))


def one_permutation(subkey):
    return jax.random.permutation(subkey, ROWS * WDEV // 128)


def draw_occupied(key, part):
    key = jax.random.fold_in(key, 11)
    blocks_total = ROWS * WDEV // 128
    subkeys = jax.random.split(key, N_TILE + 1)
    orders = jax.vmap(one_permutation)(subkeys[:N_TILE]).astype(jnp.int32)
    chosen_tile = jax.random.randint(subkeys[N_TILE], (), 0, N_TILE)
    picked_row = orders[chosen_tile]
    high_at = jnp.argmax(picked_row == blocks_total - 1).astype(jnp.int32)
    picked_row = swapped(picked_row, 0, high_at)
    low_at = jnp.argmax(picked_row == 0).astype(jnp.int32)
    picked_row = swapped(picked_row, 1, low_at)
    orders = orders.at[chosen_tile].set(picked_row)
    return orders[:, :K_SLOTS].astype(jnp.int32)


def draw_counts(key, part):
    key = jax.random.fold_in(key, 23)
    first_key, second_key = jax.random.split(key)
    drawn = jax.random.randint(first_key, (N_TILE,), K_SLOTS // 3, K_SLOTS + 1)
    full_tile = jax.random.randint(second_key, (), 0, N_TILE)
    short_tile = (full_tile + 1) % N_TILE
    positions = jnp.arange(N_TILE, dtype=jnp.int32)
    drawn = jnp.where(positions == short_tile, K_SLOTS // 3, drawn)
    return jnp.where(positions == full_tile, K_SLOTS, drawn).astype(jnp.int32)


def steps_of(key, extent, shards, low, high):
    factor_of, own = 1.0, jax.random.fold_in(key, 6)
    for dim, parts in shards:
        heights = jnp.exp(jax.random.uniform(jax.random.fold_in(own, dim), (parts,), jnp.float32, low / len(shards), high / len(shards)))
        factor_of = factor_of * jnp.repeat(heights, extent[dim] // parts).reshape([-1 if axis == dim else 1 for axis in range(len(extent))])
    return factor_of


def centred(own_key, extent, scale, limit, pieces=(), kind=jnp.bfloat16):
    values = scale * jax.random.normal(own_key, extent, jnp.float32)
    if pieces:
        values = values * steps_of(own_key, extent, pieces, -0.22, 0.18)
    return jnp.clip(values, -limit, limit).astype(kind)


def setup_inputs(seed: int = 0) -> dict:
    key_list = jax.random.split(jax.random.key(seed), 8)
    grid = centred(key_list[0], (C, FRAMES, ROWS, WIDTH), 1.0, 6.0, ((1, 8), (3, 4)))
    conv_weight = centred(key_list[1], (9, C, GROUP), (9 * GROUP) ** -0.5, 0.75)
    conv_bias = centred(key_list[2], (C,), 0.5, 3.0, (), jnp.float32)
    depth_kernel = centred(key_list[3], (LAYERS, 3, C), 0.5, 3.0, (), jnp.float32)
    point_weight = centred(key_list[4], (LAYERS, C, C), C ** -0.5, 0.75)
    occupied = draw_occupied(jax.random.fold_in(key_list[7], 71), 0)
    counts = draw_counts(jax.random.fold_in(key_list[7], 71), 0)
    return {"grid": grid, "conv_weight": conv_weight, "conv_bias": conv_bias, "depth_kernel": depth_kernel, "point_weight": point_weight, "occupied": occupied, "counts": counts}


def shifted(series, amount):
    if amount == 0:
        return series
    frames = series.shape[1]
    if amount >= frames:
        return jnp.zeros_like(series)
    leading = jnp.zeros_like(series[:, :amount])
    return jnp.concatenate([leading, series[:, :frames - amount]], axis=1)


def temporal(blocks, depth_kernel, point_weight):
    current = blocks.astype(jnp.float32)
    for layer_idx in range(depth_kernel.shape[0]):
        spacing = 2 ** layer_idx
        blended = jnp.zeros_like(current)
        for offset in range(depth_kernel.shape[1]):
            blended = blended + depth_kernel[layer_idx, offset][:, None, None, None] * shifted(current, offset * spacing)
        squashed = jax.nn.silu(blended).astype(jnp.bfloat16)
        current = current + jnp.einsum("oc,cfsn->ofsn", point_weight[layer_idx].astype(jnp.float32), squashed.astype(jnp.float32))
    return current.astype(jnp.bfloat16)


def spatial(padded, center, conv_weight, conv_bias):
    channels, frames, height, columns = center.shape
    group_count = channels // GROUP
    grouped = padded.reshape(group_count, GROUP, frames, height + 2, columns + 2).astype(jnp.float32)
    summed = jnp.zeros((group_count, GROUP, frames, height, columns), jnp.float32)
    for tap_row in range(3):
        for tap_col in range(3):
            window = grouped[:, :, :, tap_row:tap_row + height, tap_col:tap_col + columns]
            kernel = conv_weight[tap_row * 3 + tap_col].reshape(group_count, GROUP, GROUP).astype(jnp.float32)
            summed = summed + jnp.einsum("goi,gifrw->gofrw", kernel, window)
    activation = summed.reshape(channels, frames, height, columns) + conv_bias[:, None, None, None]
    return (center.astype(jnp.float32) + jax.nn.silu(activation)).astype(jnp.bfloat16)


def reference(grid, conv_weight, conv_bias, depth_kernel, point_weight, occupied, counts):
    channels, frames, height, width = grid.shape
    tile_width = width // N_TILE
    padded = jnp.pad(grid, ((0, 0), (0, 0), (1, 1), (1, 1)))

    def per_tile(tile_idx):
        tile_idx = tile_idx.astype(jnp.int32)
        strip_part = lax.dynamic_slice_in_dim(padded, tile_idx * tile_width, tile_width + 2, 3)
        center = strip_part[:, :, 1:-1, 1:-1]
        hidden = spatial(strip_part, center, conv_weight, conv_bias)
        blocks = hidden.reshape(channels, frames, height * (tile_width // 128), 128)
        block_ids = occupied[tile_idx]
        picked = jnp.take(blocks, block_ids, axis=2)
        updated = temporal(picked, depth_kernel, point_weight)
        live_slots = jnp.arange(block_ids.shape[0], dtype=jnp.int32) < counts[tile_idx]
        chosen = jnp.where(live_slots[None, None, :, None], updated, picked)
        blocks = blocks.at[:, :, block_ids].set(chosen)
        return blocks.reshape(channels, frames, height, tile_width)

    results = lax.map(per_tile, jnp.arange(N_TILE, dtype=jnp.int32))
    return results.transpose(1, 2, 3, 0, 4).reshape(channels, frames, height, width)
```

```python
import functools

import jax
import jax.numpy as jnp
from jax import lax
from jax.experimental import pallas as pl
from jax.experimental.pallas import tpu as pltpu
from jax.sharding import PartitionSpec as P

GROUP = 8
LANES = 128
MIB = 2**20


def params(mib):
    return pltpu.CompilerParams(vmem_limit_bytes=mib * MIB)


def whole(shape):
    return pl.BlockSpec(shape, lambda *_: (0,) * len(shape))


def dot(a, b, dims=((1,), (0,))):
    return lax.dot_general(a, b, (dims, ((), ())), preferred_element_type=jnp.float32)


def iota(shape, dim):
    return lax.broadcasted_iota(jnp.int32, shape, dim)


def edges_kernel(grid_ref, _, second_ref, first_ref):
    channels, frames, height, columns = grid_ref.shape
    groups, wide = channels // GROUP, GROUP * height
    count = groups * frames
    rows = iota((2 * count, columns), 0)
    lanes = iota((2 * count, columns), 1)
    even = lax.axis_index("tile") % 2 == 0
    ahead, behind = jnp.where(even, columns - 1, 0), jnp.where(even, 0, columns - 1)
    total = jnp.zeros((2 * count, wide), jnp.float32)
    for g in range(groups):
        for f in range(frames):
            at = g * frames + f
            pick = ((rows == at) & (lanes == ahead)) | ((rows == count + at) & (lanes == behind))
            cells = grid_ref[g * GROUP : (g + 1) * GROUP, f].reshape(wide, columns)
            total += dot(pick.astype(jnp.bfloat16), cells, ((1,), (1,)))
    first_ref[...] = total[:count].astype(jnp.bfloat16)
    second_ref[...] = total[count:].astype(jnp.bfloat16)


def swaps(count, start):
    partner = {i: i for i in range(count)}
    for i in range(start, count - 1, 2):
        partner[i], partner[i + 1] = i + 1, i
    return sorted(partner.items())


def edge_columns(grid, after):
    channels, frames, height, _ = grid.shape
    shape = jax.ShapeDtypeStruct((channels // GROUP * frames, GROUP * height), jnp.bfloat16)
    return pl.pallas_call(
        edges_kernel,
        in_specs=[pl.BlockSpec(memory_space=pltpu.VMEM), pl.BlockSpec(memory_space=pl.ANY)],
        out_shape=(shape, shape),
        compiler_params=params(8),
        cost_estimate=pl.CostEstimate(flops=2**28, bytes_accessed=2**21, transcendentals=0),
        name="edge_columns",
    )(grid, after)


def bands_kernel(height, taps_ref, band_ref, spread):
    _, inner, channels = taps_ref.shape
    groups, wide = channels // GROUP, GROUP * height
    repeat = (iota((inner, wide), 0) == iota((inner, wide), 1) // height).astype(jnp.bfloat16)
    offset = iota((height, wide), 1) % height - iota((height, wide), 0)
    masks = [offset == row - 1 for row in range(3)]
    for tap in range(9):
        half = (taps_ref[tap].astype(jnp.float32) * 0.5).astype(jnp.bfloat16)
        spread[tap] = dot(half, repeat, ((0,), (0,)))

    def band(g, carry):
        for col in range(3):
            rows = [spread[3 * row + col, pl.ds(pl.multiple_of(g * GROUP, GROUP), GROUP), :] for row in range(3)]
            for out in range(GROUP):
                value = jnp.zeros((height, wide), jnp.float32)
                for row in range(3):
                    value = jnp.where(masks[row], rows[row][out : out + 1], value)
                band_ref[g, out * height : (out + 1) * height, col * wide : (col + 1) * wide] = value.astype(
                    jnp.bfloat16
                )
        return carry

    lax.fori_loop(0, groups, band, 0, unroll=True)


def bands(conv_weight, height):
    taps = jnp.transpose(conv_weight, (0, 2, 1))
    channels = taps.shape[2]
    groups, wide = channels // GROUP, GROUP * height
    return pl.pallas_call(
        functools.partial(bands_kernel, height),
        out_shape=jax.ShapeDtypeStruct((groups, wide, 3 * wide), jnp.bfloat16),
        scratch_shapes=[pltpu.VMEM((9, channels, wide), jnp.float32)],
        compiler_params=params(8),
        cost_estimate=pl.CostEstimate(flops=2**28, bytes_accessed=2**23, transcendentals=0),
        name="bands",
    )(taps)


def inner_kernel(grid_ref, band_ref, summed_ref):
    channels, frames, height, columns = grid_ref.shape
    wide = GROUP * height
    lanes = iota((wide, columns), 1)

    def convolve(g, carry):
        base = pl.multiple_of(g * GROUP, GROUP)
        for f in range(frames):
            cells = grid_ref[pl.ds(base, GROUP), f].reshape(wide, columns)
            full = cells.astype(jnp.float32)
            before = jnp.where(lanes == 0, 0.0, pltpu.roll(full, 1, 1)).astype(jnp.bfloat16)
            after = jnp.where(lanes == columns - 1, 0.0, pltpu.roll(full, columns - 1, 1)).astype(jnp.bfloat16)
            summed_ref[g, f] = dot(band_ref[g], jnp.concatenate([before, cells, after], axis=0))
        return carry

    lax.fori_loop(0, channels // GROUP, convolve, 0, unroll=True)


def inner(grid, band):
    channels, frames, height, columns = grid.shape
    return pl.pallas_call(
        inner_kernel,
        out_shape=jax.ShapeDtypeStruct((channels // GROUP, frames, GROUP * height, columns), jnp.float32),
        compiler_params=params(8),
        cost_estimate=pl.CostEstimate(flops=2**31, bytes_accessed=2**23, transcendentals=0),
        name="inner",
    )(grid, band)


def steps_of(count, core_first=False):
    mixed = [(4, 2), (2, 4), (5, 3), (3, 5)] if count >= 8 else []
    seen = {0, 1} | {a for a, _ in mixed}
    across = mixed + [(d, d) for d in range(count) if d not in seen]
    return [(0, 0), (1, 1)] + across if core_first else [(0, 0)] + across + [(1, 1)]


def sent_to(me, step):
    return me ^ jnp.where(me % 2 == 0, step[0], step[1])


def got_from(me, step):
    return sent_to(me, step) if step[0] % 2 == 0 else sent_to(me, step[::-1])


def finish_kernel(occupied_ref, bias_ref, grid_ref, band_ref, summed_ref, second_ref, first_ref, hidden_ref, *rest):
    message_refs, (pick_ref, side_ref) = rest[:-2], rest[-2:]
    me = lax.axis_index("frame")
    channels, frames, height, columns = grid_ref.shape
    halves = columns // LANES
    wide = GROUP * height
    slots = occupied_ref.shape[1] // len(message_refs)
    part = GROUP * slots
    rows, lanes = iota((part, wide), 0), iota((part, wide), 1)
    at_slot, at_side = rows % slots, iota((part, LANES), 0) % slots
    same_channel, at_row = lanes // height == rows // slots, lanes % height
    for d, step in enumerate(steps_of(len(message_refs))):
        row, side = jnp.zeros((part, wide), jnp.int32), jnp.zeros((part, LANES), jnp.int32)
        for j in range(slots):
            block = occupied_ref[0, sent_to(me, step) * slots + j]
            row = jnp.where(at_slot == j, block // halves, row)
            side = jnp.where(at_side == j, block % halves, side)
        pick_ref[d * part : (d + 1) * part, :] = (same_channel & (at_row == row)).astype(jnp.bfloat16)
        side_ref[d * part : (d + 1) * part, :] = side

    tile, tiles = lax.axis_index("tile"), lax.axis_size("tile")
    even = tile % 2 == 0
    first, second = first_ref[...].astype(jnp.float32), second_ref[...].astype(jnp.float32)
    left = jnp.where(tile > 0, jnp.where(even, second, first), 0.0)
    right = jnp.where(tile < tiles - 1, jnp.where(even, first, second), 0.0)
    rim = 16
    rim_rows = iota((rim, wide), 0)
    blank = jnp.zeros((LANES - rim, wide), jnp.bfloat16)

    def edge_terms(g):
        before, after = [], []
        for f in range(frames):
            at = slice(g * frames + f, g * frames + f + 1)
            before += [jnp.where(rim_rows == 0, left[at], 0.0).astype(jnp.bfloat16), blank]
            after += [blank, jnp.where(rim_rows == rim - 1, right[at], 0.0).astype(jnp.bfloat16)]
        return (
            dot(band_ref[g, :, :wide], jnp.concatenate(before, axis=0), ((1,), (1,))),
            dot(band_ref[g, :, 2 * wide :], jnp.concatenate(after, axis=0), ((1,), (1,))),
        )

    def activate(g):
        at_left, at_right = edge_terms(g)
        for f in range(frames):
            across = slice(f * LANES, (f + 1) * LANES)
            for out in range(GROUP):
                c = g * GROUP + out
                part = slice(out * height, (out + 1) * height)
                half = summed_ref[g, f, part, :] + 0.5 * bias_ref[c]
                tiles = [half[:, side * LANES : (side + 1) * LANES] for side in range(halves)]
                tiles[0] += at_left[part, across]
                tiles[-1] += at_right[part, across]
                half = jnp.concatenate(tiles, axis=1)
                hidden = grid_ref[c, f].astype(jnp.float32) + (half + half * jnp.tanh(half))
                hidden_ref[c, f] = hidden.astype(jnp.bfloat16)

    def pick(g):
        for f in range(frames):
            picked = dot(pick_ref[...], hidden_ref[g * GROUP : (g + 1) * GROUP, f].reshape(wide, columns))
            chosen = picked[:, :LANES]
            for side in range(1, halves):
                chosen = jnp.where(side_ref[...] == side, picked[:, side * LANES : (side + 1) * LANES], chosen)
            chosen = chosen.astype(jnp.bfloat16)
            for d, message_ref in enumerate(message_refs):
                message_ref[f, g * part : (g + 1) * part, :] = chosen[d * part : (d + 1) * part]

    groups = channels // GROUP
    for g in range(groups + 1):
        if g < groups:
            activate(g)
        if g > 0:
            pick(g - 1)


def finish(grid, band, summed, conv_bias, second, first, occupied, parts):
    channels, frames, height, columns = grid.shape
    slots = occupied.shape[1] // parts
    smem, vmem = pl.BlockSpec(memory_space=pltpu.SMEM), pl.BlockSpec(memory_space=pltpu.VMEM)
    return pl.pallas_call(
        finish_kernel,
        in_specs=[smem, smem, vmem, vmem, vmem, vmem, vmem],
        out_shape=[jax.ShapeDtypeStruct(grid.shape, jnp.bfloat16)]
        + [jax.ShapeDtypeStruct((frames, channels * slots, LANES), jnp.bfloat16)] * parts,
        scratch_shapes=[
            pltpu.VMEM((parts * GROUP * slots, GROUP * height), jnp.bfloat16),
            pltpu.VMEM((parts * GROUP * slots, LANES), jnp.int32),
        ],
        compiler_params=params(8),
        cost_estimate=pl.CostEstimate(flops=2**30, bytes_accessed=2**23, transcendentals=2**20),
        name="finish",
    )(occupied, conv_bias, grid, band, summed, second, first)


def tables_kernel(depth_ref, point_ref, _, table_ref, mix_ref):
    layers, channels, _ = point_ref.shape
    taps = depth_ref.shape[0]
    tall = mix_ref.shape[1]
    slots = tall // channels
    same_channel = iota((tall, channels), 0) // slots == iota((tall, channels), 1)
    up = same_channel.astype(jnp.bfloat16)
    across = (iota((channels, tall), 1) // slots == iota((channels, tall), 0)).astype(jnp.bfloat16)
    same_slot = iota((tall, tall), 0) % slots == iota((tall, tall), 1) % slots
    for layer in range(layers):
        for tap in range(taps):
            row = 0.5 * depth_ref[tap, layer : layer + 1, :]
            column = jnp.sum(jnp.where(same_channel, row, 0.0), axis=1, keepdims=True)
            table_ref[layer * taps + tap] = jnp.broadcast_to(column, table_ref.shape[1:])
        spread = dot(dot(up, point_ref[layer]).astype(jnp.bfloat16), across)
        mix_ref[layer] = jnp.where(same_slot, spread, 0.0).astype(jnp.bfloat16)


def tables(depth_kernel, point_weight, slots, after):
    layers, taps, channels = depth_kernel.shape
    vmem = pl.BlockSpec(memory_space=pltpu.VMEM)
    return pl.pallas_call(
        tables_kernel,
        in_specs=[vmem, vmem, pl.BlockSpec(memory_space=pl.ANY)],
        out_shape=(
            jax.ShapeDtypeStruct((layers * taps, channels * slots, LANES), jnp.float32),
            jax.ShapeDtypeStruct((layers, channels * slots, channels * slots), jnp.bfloat16),
        ),
        compiler_params=params(8),
        cost_estimate=pl.CostEstimate(flops=2**27, bytes_accessed=2**22, transcendentals=0),
        name="tables",
    )(jnp.transpose(depth_kernel, (1, 0, 2)), point_weight, after)


def temporal_kernel(sources, depth_ref, mix_ref, *refs):
    message_refs, out_refs = refs[:sources], refs[sources : 2 * sources]
    state, squashed, final = refs[2 * sources :]
    me = lax.axis_index("frame")
    local, tall, lanes = message_refs[0].shape
    frames = sources * local
    layers = mix_ref.shape[0]
    taps = depth_ref.shape[0] // layers
    quads, _, width = squashed.shape
    quad = width // lanes
    for step, message_ref in zip(steps_of(sources), message_refs):
        for f in range(local):
            state[got_from(me, step) * local + f] = message_ref[f].astype(jnp.float32)
    height = 32
    for layer in range(layers):
        spacing = 2**layer
        for q in reversed(range(quads)):
            inside = range(q * quad, (q + 1) * quad)
            for top in range(0, tall, height):
                part = slice(top, top + height)
                scale = [depth_ref[layer * taps + tap, part] for tap in range(taps)]
                needed = {f - tap * spacing for f in inside for tap in range(taps)}
                series = {f: state[f, part] for f in needed if f >= 0}
                for f in inside:
                    half = scale[0] * series[f]
                    for tap in range(1, taps):
                        if f >= tap * spacing:
                            half += scale[tap] * series[f - tap * spacing]
                    across = slice((f - q * quad) * lanes, (f - q * quad + 1) * lanes)
                    squashed[q, part, across] = (half + half * jnp.tanh(half)).astype(jnp.bfloat16)
            mixed = dot(mix_ref[layer], squashed[q])
            for f in inside:
                after = state[f] + mixed[:, (f - q * quad) * lanes : (f - q * quad + 1) * lanes]
                if layer + 1 < layers:
                    state[f] = after
                else:
                    final[f] = after.astype(jnp.bfloat16)
    for step, out_ref in zip(steps_of(sources, True), out_refs):
        for f in range(local):
            out_ref[f] = final[sent_to(me, step) * local + f]


def temporal(messages, depth, mix):
    sources = len(messages)
    local, tall, lanes = messages[0].shape
    vmem = pl.BlockSpec(memory_space=pltpu.VMEM)
    return pl.pallas_call(
        functools.partial(temporal_kernel, sources),
        in_specs=[vmem, vmem] + [vmem] * sources,
        out_shape=[jax.ShapeDtypeStruct(messages[0].shape, jnp.bfloat16)] * sources,
        scratch_shapes=[
            pltpu.VMEM((sources * local, tall, lanes), jnp.float32),
            pltpu.VMEM((sources * local // 4, tall, 4 * lanes), jnp.bfloat16),
            pltpu.VMEM((sources * local, tall, lanes), jnp.bfloat16),
        ],
        compiler_params=params(12),
        cost_estimate=pl.CostEstimate(flops=2**30, bytes_accessed=2**21, transcendentals=2**21),
        name="temporal",
    )(depth, mix, *messages)


def plan_kernel(sources, occupied_ref, counts_ref, _, put_ref, cover_ref):
    me = lax.axis_index("frame")
    halves, wide, tall = put_ref.shape
    part = tall // sources
    slots = part // GROUP
    height = wide // GROUP
    rows, lanes = iota((part, wide), 0), iota((part, wide), 1)
    same_channel, at_slot, at_row = lanes // height == rows // slots, rows % slots, lanes % height
    for side in range(halves):
        hits = []
        for step in steps_of(sources, True):
            row = jnp.full((part, wide), -1, jnp.int32)
            for j in range(slots):
                slot = got_from(me, step) * slots + j
                block = occupied_ref[0, slot]
                used = (slot < counts_ref[0]) & (block % halves == side)
                row = jnp.where(at_slot == j, jnp.where(used, block // halves, -1), row)
            hits.append((same_channel & (at_row == row)).astype(jnp.float32))
        put = jnp.transpose(jnp.concatenate(hits, axis=0)).astype(jnp.bfloat16)
        put_ref[side] = put
        cover_ref[side] = dot(put, jnp.ones((tall, LANES), jnp.bfloat16))


def plan(occupied, counts, wide, halves, sources, after):
    smem = pl.BlockSpec(memory_space=pltpu.SMEM)
    return pl.pallas_call(
        functools.partial(plan_kernel, sources),
        in_specs=[smem, smem, pl.BlockSpec(memory_space=pl.ANY)],
        out_shape=(
            jax.ShapeDtypeStruct((halves, wide, GROUP * occupied.shape[1]), jnp.bfloat16),
            jax.ShapeDtypeStruct((halves, wide, LANES), jnp.float32),
        ),
        compiler_params=params(8),
        cost_estimate=pl.CostEstimate(flops=2**27, bytes_accessed=2**22, transcendentals=0),
        name="plan",
    )(occupied, counts, after)


def place_kernel(sources, put_ref, cover_ref, hidden_ref, *refs):
    message_refs, (out_hbm, out_ref, sems) = refs[:sources], refs[sources:]
    channels, frames, height, columns = hidden_ref.shape
    halves = columns // LANES
    wide = GROUP * height
    part = put_ref.shape[2] // sources

    def group_copy(g):
        cells = pl.ds(pl.multiple_of(g * GROUP, GROUP), GROUP)
        return pltpu.make_async_copy(out_ref.at[cells], out_hbm.at[cells], sems.at[g])

    def merge(g, carry):
        base = pl.multiple_of(g * GROUP, GROUP)
        rows_of = pl.ds(pl.multiple_of(g * part, part), part)
        updated = jnp.concatenate(
            [
                jnp.concatenate([ref[f, rows_of, :] for f in range(frames)], axis=1)
                for ref in message_refs
            ],
            axis=0,
        )
        for side in range(halves):
            spread = dot(put_ref[side], updated)
            across = slice(side * LANES, (side + 1) * LANES)
            for f in range(frames):
                cells = hidden_ref[pl.ds(base, GROUP), f, :, across].reshape(wide, LANES).astype(jnp.float32)
                merged = jnp.where(cover_ref[side] > 0.5, spread[:, f * LANES : (f + 1) * LANES], cells)
                out_ref[pl.ds(base, GROUP), f, :, across] = merged.astype(jnp.bfloat16).reshape(GROUP, height, LANES)
        group_copy(g).start()
        return carry

    groups = channels // GROUP
    lax.fori_loop(0, groups, merge, 0, unroll=True)
    for g in range(groups):
        group_copy(g).wait()


def place(hidden, messages, put, cover):
    channels = hidden.shape[0]
    sources = len(messages)
    vmem, anywhere = pl.BlockSpec(memory_space=pltpu.VMEM), pl.BlockSpec(memory_space=pl.ANY)
    return pl.pallas_call(
        functools.partial(place_kernel, sources),
        in_specs=[vmem, vmem, vmem] + [vmem] * sources,
        out_specs=anywhere,
        out_shape=jax.ShapeDtypeStruct(hidden.shape, jnp.bfloat16),
        scratch_shapes=[
            pltpu.VMEM(hidden.shape, jnp.bfloat16),
            pltpu.SemaphoreType.DMA((channels // GROUP,)),
        ],
        compiler_params=params(8),
        cost_estimate=pl.CostEstimate(flops=2**28, bytes_accessed=2**22, transcendentals=0),
        name="place",
    )(put, cover, hidden, *messages)


def exchange(arrays, core_first):
    count = len(arrays)
    return [
        array if step == (0, 0) else lax.ppermute(array, "frame", [(i, i ^ step[i % 2]) for i in range(count)])
        for array, step in zip(arrays, steps_of(count, core_first))
    ]


def on_device(grid, conv_weight, conv_bias, depth_kernel, point_weight, occupied, counts):
    channels, frames, height, columns = grid.shape
    tiles, parts = lax.axis_size("tile"), lax.axis_size("frame")
    slots = occupied.shape[1] // parts
    band = bands(conv_weight, height)
    second, first = edge_columns(grid, band)
    second = lax.ppermute(second, "tile", swaps(tiles, 1))
    first = lax.ppermute(first, "tile", swaps(tiles, 0))
    summed = inner(grid, band)
    hidden, *messages = finish(grid, band, summed, conv_bias, second, first, occupied, parts)
    depth, mix = tables(depth_kernel, point_weight, slots, messages[0])
    updated = temporal(exchange(messages, False), depth, mix)
    put, cover = plan(occupied, counts, GROUP * height, columns // LANES, parts, updated[0])
    return place(hidden, exchange(updated, True), put, cover)


def solution(mesh):
    placed = (P(None, "frame", None, "tile"), P(), P(), P(), P(), P("tile", None), P("tile"))
    return jax.shard_map(
        on_device,
        mesh=mesh,
        in_specs=placed,
        out_specs=P(None, "frame", None, "tile"),
        check_vma=False,
    )
```

```python
import functools

import jax
import jax.numpy as jnp
from jax import lax
from jax.experimental import pallas as pl
from jax.experimental.pallas import tpu as pltpu
from jax.sharding import PartitionSpec as P

GROUP = 8
LANES = 128
MIB = 2**20
ROLLED = jnp.bfloat16


def params(mib):
    return pltpu.CompilerParams(vmem_limit_bytes=mib * MIB)


def whole(shape):
    return pl.BlockSpec(shape, lambda *_: (0,) * len(shape))


def dot(a, b, dims=((1,), (0,))):
    return lax.dot_general(a, b, (dims, ((), ())), preferred_element_type=jnp.float32)


def iota(shape, dim):
    return lax.broadcasted_iota(jnp.int32, shape, dim)


def edges_kernel(grid_ref, _, first_ref, second_ref):
    channels, frames, height, columns = grid_ref.shape
    groups, wide = channels // GROUP, GROUP * height
    count = groups * frames
    rows = iota((2 * count, columns), 0)
    lanes = iota((2 * count, columns), 1)
    even = lax.axis_index("tile") % 2 == 0
    ahead, behind = jnp.where(even, columns - 1, 0), jnp.where(even, 0, columns - 1)
    total = jnp.zeros((2 * count, wide), jnp.float32)
    for g in range(groups):
        for f in range(frames):
            at = g * frames + f
            pick = ((rows == at) & (lanes == ahead)) | ((rows == count + at) & (lanes == behind))
            cells = grid_ref[g * GROUP : (g + 1) * GROUP, f].reshape(wide, columns)
            total += dot(pick.astype(jnp.bfloat16), cells, ((1,), (1,)))
    first_ref[...] = total[:count].astype(jnp.bfloat16)
    second_ref[...] = total[count:].astype(jnp.bfloat16)


def swaps(count, start):
    partner = {i: i for i in range(count)}
    for i in range(start, count - 1, 2):
        partner[i], partner[i + 1] = i + 1, i
    return sorted(partner.items())


def edge_columns(grid, after):
    channels, frames, height, _ = grid.shape
    shape = jax.ShapeDtypeStruct((channels // GROUP * frames, GROUP * height), jnp.bfloat16)
    return pl.pallas_call(
        edges_kernel,
        in_specs=[pl.BlockSpec(memory_space=pltpu.VMEM), pl.BlockSpec(memory_space=pl.ANY)],
        out_shape=(shape, shape),
        compiler_params=params(8),
        cost_estimate=pl.CostEstimate(flops=2**28, bytes_accessed=2**21, transcendentals=0),
        name="edge_columns",
    )(grid, after)


def bands_kernel(height, taps_ref, band_ref, spread):
    _, inner, channels = taps_ref.shape
    groups, wide = channels // GROUP, GROUP * height
    repeat = (iota((inner, wide), 0) == iota((inner, wide), 1) // height).astype(jnp.bfloat16)
    offset = iota((height, wide), 1) % height - iota((height, wide), 0)
    masks = [offset == row - 1 for row in range(3)]
    for tap in range(9):
        half = (taps_ref[tap].astype(jnp.float32) * 0.5).astype(jnp.bfloat16)
        spread[tap] = dot(half, repeat, ((0,), (0,)))

    def band(g, carry):
        for col in range(3):
            rows = [spread[3 * row + col, pl.ds(pl.multiple_of(g * GROUP, GROUP), GROUP), :] for row in range(3)]
            for out in range(GROUP):
                value = jnp.zeros((height, wide), jnp.float32)
                for row in range(3):
                    value = jnp.where(masks[row], rows[row][out : out + 1], value)
                band_ref[g, out * height : (out + 1) * height, col * wide : (col + 1) * wide] = value.astype(
                    jnp.bfloat16
                )
        return carry

    lax.fori_loop(0, groups, band, 0)


def bands(conv_weight, height):
    taps = jnp.transpose(conv_weight, (0, 2, 1))
    channels = taps.shape[2]
    groups, wide = channels // GROUP, GROUP * height
    return pl.pallas_call(
        functools.partial(bands_kernel, height),
        out_shape=jax.ShapeDtypeStruct((groups, wide, 3 * wide), jnp.bfloat16),
        scratch_shapes=[pltpu.VMEM((9, channels, wide), jnp.float32)],
        compiler_params=params(8),
        cost_estimate=pl.CostEstimate(flops=2**28, bytes_accessed=2**23, transcendentals=0),
        name="bands",
    )(taps)


def inner_kernel(occupied_ref, bias_ref, grid_ref, band_ref, summed_ref, cells_ref, pick_ref, side_ref):
    channels, frames, height, columns = grid_ref.shape
    halves = columns // LANES
    wide = GROUP * height
    me, count = lax.axis_index("frame"), lax.axis_size("frame")
    slots = occupied_ref.shape[1] // count
    part = GROUP * slots
    rows, lanes = iota((part, wide), 0), iota((part, wide), 1)
    at_slot, at_side = rows % slots, iota((part, LANES), 0) % slots
    same_channel, at_row = lanes // height == rows // slots, lanes % height
    for d, step in enumerate(steps_of(count)):
        row, side = jnp.zeros((part, wide), jnp.int32), jnp.zeros((part, LANES), jnp.int32)
        for j in range(slots):
            block = occupied_ref[0, sent_to(me, step) * slots + j]
            row = jnp.where(at_slot == j, block // halves, row)
            side = jnp.where(at_side == j, block % halves, side)
        pick_ref[d * part : (d + 1) * part, :] = (same_channel & (at_row == row)).astype(jnp.bfloat16)
        side_ref[d * part : (d + 1) * part, :] = side

    tile_lanes = iota((wide, LANES), 1)
    is_first, is_last = tile_lanes == 0, tile_lanes == LANES - 1
    nothing = jnp.zeros((wide, LANES), ROLLED)

    def shifted(g, f):
        cells = grid_ref[g * GROUP : (g + 1) * GROUP, f].reshape(wide, columns)
        tiles = [cells[:, side * LANES : (side + 1) * LANES].astype(ROLLED) for side in range(halves)]
        right = [pltpu.roll(tile, 1, 1) for tile in tiles]
        left = [pltpu.roll(tile, LANES - 1, 1) for tile in tiles]
        before = [jnp.where(is_first, *pair) for pair in zip([nothing] + right[:-1], right)]
        after = [jnp.where(is_last, *pair) for pair in zip(left[1:] + [nothing], left)]
        join = lambda parts: jnp.concatenate(parts, axis=1).astype(jnp.bfloat16)
        return jnp.concatenate([join(before), cells, join(after)], axis=0)

    items = [(g, f) for g in range(channels // GROUP) for f in range(frames)]
    ready = shifted(*items[0])
    for (g, f), following in zip(items, items[1:] + [None]):
        summed = dot(band_ref[g], ready)
        if following is not None:
            ready = shifted(*following)
        for out in range(GROUP):
            inside = slice(out * height, (out + 1) * height)
            summed_ref[g, f, inside, :] = summed[inside] + 0.5 * bias_ref[g * GROUP + out]
            cells_ref[g, f, inside, :] = grid_ref[g * GROUP + out, f].astype(jnp.float32)


def inner(grid, band, conv_bias, occupied, parts):
    channels, frames, height, columns = grid.shape
    part = GROUP * (occupied.shape[1] // parts)
    smem, vmem = pl.BlockSpec(memory_space=pltpu.SMEM), pl.BlockSpec(memory_space=pltpu.VMEM)
    wide = jax.ShapeDtypeStruct((channels // GROUP, frames, GROUP * height, columns), jnp.float32)
    return pl.pallas_call(
        inner_kernel,
        in_specs=[smem, smem, vmem, vmem],
        out_shape=(
            wide,
            wide,
            jax.ShapeDtypeStruct((parts * part, GROUP * height), jnp.bfloat16),
            jax.ShapeDtypeStruct((parts * part, LANES), jnp.int32),
        ),
        compiler_params=params(8),
        cost_estimate=pl.CostEstimate(flops=2**31, bytes_accessed=2**23, transcendentals=0),
        name="inner",
    )(occupied, conv_bias, grid, band)


def steps_of(count, core_first=False):
    mixed = [(4, 2), (2, 4), (5, 3), (3, 5)] if count >= 8 else []
    seen = {0, 1} | {a for a, _ in mixed}
    across = mixed + [(d, d) for d in range(count) if d not in seen]
    return [(0, 0), (1, 1)] + across if core_first else [(0, 0)] + across + [(1, 1)]


def sent_to(me, step):
    return me ^ jnp.where(me % 2 == 0, step[0], step[1])


def got_from(me, step):
    return sent_to(me, step) if step[0] % 2 == 0 else sent_to(me, step[::-1])


def finish_kernel(band_ref, summed_ref, cells_ref, pick_ref, side_ref, first_ref, second_ref, hidden_ref, *message_refs):
    channels, frames, height, columns = hidden_ref.shape
    halves = columns // LANES
    wide = GROUP * height
    part = pick_ref.shape[0] // len(message_refs)
    tile, tiles = lax.axis_index("tile"), lax.axis_size("tile")
    even = tile % 2 == 0
    first, second = first_ref[...].astype(jnp.float32), second_ref[...].astype(jnp.float32)
    left = jnp.where(tile > 0, jnp.where(even, second, first), 0.0)
    right = jnp.where(tile < tiles - 1, jnp.where(even, first, second), 0.0)
    rim = 16
    rim_rows = iota((rim, wide), 0)
    blank = jnp.zeros((LANES - rim, wide), jnp.bfloat16)

    def edge_terms(g):
        before, after = [], []
        for f in range(frames):
            at = slice(g * frames + f, g * frames + f + 1)
            before += [jnp.where(rim_rows == 0, left[at], 0.0).astype(jnp.bfloat16), blank]
            after += [blank, jnp.where(rim_rows == rim - 1, right[at], 0.0).astype(jnp.bfloat16)]
        return (
            dot(band_ref[g, :, :wide], jnp.concatenate(before, axis=0), ((1,), (1,))),
            dot(band_ref[g, :, 2 * wide :], jnp.concatenate(after, axis=0), ((1,), (1,))),
        )

    def activate(g, at_left, at_right):
        for f in range(frames):
            across = slice(f * LANES, (f + 1) * LANES)
            for out in range(GROUP):
                c = g * GROUP + out
                part = slice(out * height, (out + 1) * height)
                half = summed_ref[g, f, part, :]
                tiles = [half[:, side * LANES : (side + 1) * LANES] for side in range(halves)]
                tiles[0] += at_left[part, across]
                tiles[-1] += at_right[part, across]
                half = jnp.concatenate(tiles, axis=1)
                hidden = cells_ref[g, f, part, :] + (half + half * jnp.tanh(half))
                hidden_ref[c, f] = hidden.astype(jnp.bfloat16)

    def pick(g):
        return [
            dot(pick_ref[...], hidden_ref[g * GROUP : (g + 1) * GROUP, f].reshape(wide, columns))
            for f in range(frames)
        ]

    def send(g, picks):
        for f, picked in enumerate(picks):
            chosen = picked[:, :LANES]
            for side in range(1, halves):
                chosen = jnp.where(side_ref[...] == side, picked[:, side * LANES : (side + 1) * LANES], chosen)
            chosen = chosen.astype(jnp.bfloat16)
            for d, message_ref in enumerate(message_refs):
                message_ref[f, g * part : (g + 1) * part, :] = chosen[d * part : (d + 1) * part]

    groups = channels // GROUP
    terms = edge_terms(0)
    for g in range(groups):
        current = terms
        picks = pick(g - 1) if g > 0 else None
        terms = edge_terms(g + 1) if g + 1 < groups else None
        activate(g, *current)
        if picks is not None:
            send(g - 1, picks)
    send(groups - 1, pick(groups - 1))


def finish(grid, band, summed, cells, pick, side, first, second, parts):
    channels, frames, _, _ = grid.shape
    slots = pick.shape[0] // (GROUP * parts)
    vmem = pl.BlockSpec(memory_space=pltpu.VMEM)
    return pl.pallas_call(
        finish_kernel,
        in_specs=[vmem] * 7,
        out_shape=[jax.ShapeDtypeStruct(grid.shape, jnp.bfloat16)]
        + [jax.ShapeDtypeStruct((frames, channels * slots, LANES), jnp.bfloat16)] * parts,
        compiler_params=params(8),
        cost_estimate=pl.CostEstimate(flops=2**30, bytes_accessed=2**23, transcendentals=2**20),
        name="finish",
    )(band, summed, cells, pick, side, first, second)


def tables_kernel(depth_ref, point_ref, _, table_ref, mix_ref):
    layers, channels, _ = point_ref.shape
    taps = depth_ref.shape[0]
    tall = mix_ref.shape[1]
    slots = tall // channels
    same_channel = iota((tall, channels), 0) // slots == iota((tall, channels), 1)
    up = same_channel.astype(jnp.bfloat16)
    across = (iota((channels, tall), 1) // slots == iota((channels, tall), 0)).astype(jnp.bfloat16)
    same_slot = iota((tall, tall), 0) % slots == iota((tall, tall), 1) % slots
    for layer in range(layers):
        for tap in range(taps):
            row = 0.5 * depth_ref[tap, layer : layer + 1, :]
            column = jnp.sum(jnp.where(same_channel, row, 0.0), axis=1, keepdims=True)
            table_ref[layer * taps + tap] = jnp.broadcast_to(column, table_ref.shape[1:])
        spread = dot(dot(up, point_ref[layer]).astype(jnp.bfloat16), across)
        mix_ref[layer] = jnp.where(same_slot, spread, 0.0).astype(jnp.bfloat16)


def tables(depth_kernel, point_weight, slots, after):
    layers, taps, channels = depth_kernel.shape
    vmem = pl.BlockSpec(memory_space=pltpu.VMEM)
    return pl.pallas_call(
        tables_kernel,
        in_specs=[vmem, vmem, pl.BlockSpec(memory_space=pl.ANY)],
        out_shape=(
            jax.ShapeDtypeStruct((layers * taps, channels * slots, LANES), jnp.float32),
            jax.ShapeDtypeStruct((layers, channels * slots, channels * slots), jnp.bfloat16),
        ),
        compiler_params=params(8),
        cost_estimate=pl.CostEstimate(flops=2**27, bytes_accessed=2**22, transcendentals=0),
        name="tables",
    )(jnp.transpose(depth_kernel, (1, 0, 2)), point_weight, after)


def temporal_kernel(sources, depth_ref, mix_ref, *refs):
    message_refs, out_refs = refs[:sources], refs[sources : 2 * sources]
    state, squashed, final = refs[2 * sources :]
    me = lax.axis_index("frame")
    local, tall, lanes = message_refs[0].shape
    frames = sources * local
    layers = mix_ref.shape[0]
    taps = depth_ref.shape[0] // layers
    quads, _, width = squashed.shape
    quad = width // lanes
    for step, message_ref in zip(steps_of(sources), message_refs):
        for f in range(local):
            state[got_from(me, step) * local + f] = message_ref[f].astype(jnp.float32)
    height = 32

    def blend(layer, q):
        spacing = 2**layer
        inside = range(q * quad, (q + 1) * quad)
        for top in range(0, tall, height):
            part = slice(top, top + height)
            scale = [depth_ref[layer * taps + tap, part] for tap in range(taps)]
            needed = {f - tap * spacing for f in inside for tap in range(taps)}
            series = {f: state[f, part] for f in sorted(needed) if f >= 0}
            for f in inside:
                half = scale[0] * series[f]
                for tap in range(1, taps):
                    if f >= tap * spacing:
                        half += scale[tap] * series[f - tap * spacing]
                across = slice((f - q * quad) * lanes, (f - q * quad + 1) * lanes)
                squashed[q, part, across] = (half + half * jnp.tanh(half)).astype(jnp.bfloat16)

    def update(layer, q, mixed):
        for f in range(q * quad, (q + 1) * quad):
            after = state[f] + mixed[:, (f - q * quad) * lanes : (f - q * quad + 1) * lanes]
            if layer + 1 < layers:
                state[f] = after
            else:
                final[f] = after.astype(jnp.bfloat16)

    waiting = None
    for layer in range(layers):
        for q in reversed(range(quads)):
            reads = {(f - tap * 2**layer) // quad for f in range(q * quad, (q + 1) * quad) for tap in range(taps)}
            late = waiting is not None and waiting[1] not in reads
            if waiting is not None and not late:
                update(*waiting)
            blend(layer, q)
            if late:
                update(*waiting)
            waiting = layer, q, dot(mix_ref[layer], squashed[q])
    update(*waiting)
    for step, out_ref in zip(steps_of(sources, True), out_refs):
        for f in range(local):
            out_ref[f] = final[sent_to(me, step) * local + f]


def temporal(messages, depth, mix):
    sources = len(messages)
    local, tall, lanes = messages[0].shape
    vmem = pl.BlockSpec(memory_space=pltpu.VMEM)
    return pl.pallas_call(
        functools.partial(temporal_kernel, sources),
        in_specs=[vmem, vmem] + [vmem] * sources,
        out_shape=[jax.ShapeDtypeStruct(messages[0].shape, jnp.bfloat16)] * sources,
        scratch_shapes=[
            pltpu.VMEM((sources * local, tall, lanes), jnp.float32),
            pltpu.VMEM((sources * local // 4, tall, 4 * lanes), jnp.bfloat16),
            pltpu.VMEM((sources * local, tall, lanes), jnp.bfloat16),
        ],
        compiler_params=params(12),
        cost_estimate=pl.CostEstimate(flops=2**30, bytes_accessed=2**21, transcendentals=2**21),
        name="temporal",
    )(depth, mix, *messages)


def plan_kernel(sources, occupied_ref, counts_ref, _, put_ref, cover_ref):
    me = lax.axis_index("frame")
    halves, wide, tall = put_ref.shape
    part = tall // sources
    slots = part // GROUP
    height = wide // GROUP
    rows, lanes = iota((part, wide), 0), iota((part, wide), 1)
    same_channel, at_slot, at_row = lanes // height == rows // slots, rows % slots, lanes % height
    for side in range(halves):
        hits = []
        for step in steps_of(sources, True):
            row = jnp.full((part, wide), -1, jnp.int32)
            for j in range(slots):
                slot = got_from(me, step) * slots + j
                block = occupied_ref[0, slot]
                used = (slot < counts_ref[0]) & (block % halves == side)
                row = jnp.where(at_slot == j, jnp.where(used, block // halves, -1), row)
            hits.append((same_channel & (at_row == row)).astype(jnp.float32))
        put = jnp.transpose(jnp.concatenate(hits, axis=0)).astype(jnp.bfloat16)
        put_ref[side] = put
        cover_ref[side] = dot(put, jnp.ones((tall, LANES), jnp.bfloat16))


def plan(occupied, counts, wide, halves, sources, after):
    smem = pl.BlockSpec(memory_space=pltpu.SMEM)
    return pl.pallas_call(
        functools.partial(plan_kernel, sources),
        in_specs=[smem, smem, pl.BlockSpec(memory_space=pl.ANY)],
        out_shape=(
            jax.ShapeDtypeStruct((halves, wide, GROUP * occupied.shape[1]), jnp.bfloat16),
            jax.ShapeDtypeStruct((halves, wide, LANES), jnp.float32),
        ),
        compiler_params=params(8),
        cost_estimate=pl.CostEstimate(flops=2**27, bytes_accessed=2**22, transcendentals=0),
        name="plan",
    )(occupied, counts, after)


def place_kernel(sources, put_ref, cover_ref, hidden_ref, *refs):
    message_refs, (out_hbm, out_ref, sems) = refs[:sources], refs[sources:]
    channels, frames, height, columns = hidden_ref.shape
    halves = columns // LANES
    wide = GROUP * height
    part = put_ref.shape[2] // sources

    def group_copy(g):
        cells = pl.ds(g * GROUP, GROUP)
        return pltpu.make_async_copy(out_ref.at[cells], out_hbm.at[cells], sems.at[g])

    def spread(g):
        rows = slice(g * part, (g + 1) * part)
        updated = jnp.concatenate(
            [jnp.concatenate([ref[f, rows, :] for f in range(frames)], axis=1) for ref in message_refs], axis=0
        )
        return [dot(put_ref[side], updated) for side in range(halves)]

    def merge(g, spreads):
        base = g * GROUP
        for side in range(halves):
            across = slice(side * LANES, (side + 1) * LANES)
            for f in range(frames):
                cells = hidden_ref[base : base + GROUP, f, :, across].reshape(wide, LANES).astype(jnp.float32)
                merged = jnp.where(cover_ref[side] > 0.5, spreads[side][:, f * LANES : (f + 1) * LANES], cells)
                out_ref[base : base + GROUP, f, :, across] = merged.astype(jnp.bfloat16).reshape(GROUP, height, LANES)
        group_copy(g).start()

    groups = channels // GROUP
    following = spread(0)
    for g in range(groups):
        current = following
        following = spread(g + 1) if g + 1 < groups else None
        merge(g, current)
    for g in range(groups):
        group_copy(g).wait()


def place(hidden, messages, put, cover):
    channels = hidden.shape[0]
    sources = len(messages)
    vmem, anywhere = pl.BlockSpec(memory_space=pltpu.VMEM), pl.BlockSpec(memory_space=pl.ANY)
    return pl.pallas_call(
        functools.partial(place_kernel, sources),
        in_specs=[vmem, vmem, vmem] + [vmem] * sources,
        out_specs=anywhere,
        out_shape=jax.ShapeDtypeStruct(hidden.shape, jnp.bfloat16),
        scratch_shapes=[
            pltpu.VMEM(hidden.shape, jnp.bfloat16),
            pltpu.SemaphoreType.DMA((channels // GROUP,)),
        ],
        compiler_params=params(8),
        cost_estimate=pl.CostEstimate(flops=2**28, bytes_accessed=2**22, transcendentals=0),
        name="place",
    )(put, cover, hidden, *messages)


def exchange(arrays, core_first):
    count = len(arrays)
    return [
        array if step == (0, 0) else lax.ppermute(array, "frame", [(i, i ^ step[i % 2]) for i in range(count)])
        for array, step in zip(arrays, steps_of(count, core_first))
    ]


def on_device(grid, conv_weight, conv_bias, depth_kernel, point_weight, occupied, counts):
    channels, frames, height, columns = grid.shape
    tiles, parts = lax.axis_size("tile"), lax.axis_size("frame")
    slots = occupied.shape[1] // parts
    band = bands(conv_weight, height)
    first, second = edge_columns(grid, band)
    first = lax.ppermute(first, "tile", swaps(tiles, 0))
    second = lax.ppermute(second, "tile", swaps(tiles, 1))
    inside = inner(grid, band, conv_bias, occupied, parts)
    hidden, *messages = finish(grid, band, *inside, first, second, parts)
    depth, mix = tables(depth_kernel, point_weight, slots, messages[0])
    updated = temporal(exchange(messages, False), depth, mix)
    put, cover = plan(occupied, counts, GROUP * height, columns // LANES, parts, updated[0])
    return place(hidden, exchange(updated, True), put, cover)


def solution(mesh):
    placed = (P(None, "frame", None, "tile"), P(), P(), P(), P(), P("tile", None), P("tile"))
    return jax.shard_map(
        on_device,
        mesh=mesh,
        in_specs=placed,
        out_specs=P(None, "frame", None, "tile"),
        check_vma=False,
    )
```

```python
import functools

import jax
import jax.numpy as jnp
from jax import lax
from jax.experimental import pallas as pl
from jax.experimental.pallas import tpu as pltpu
from jax.sharding import PartitionSpec as P

GROUP = 8
LANES = 128
MIB = 2**20


def params(mib):
    return pltpu.CompilerParams(vmem_limit_bytes=mib * MIB)


def whole(shape):
    return pl.BlockSpec(shape, lambda *_: (0,) * len(shape))


def dot(a, b, dims=((1,), (0,))):
    return lax.dot_general(a, b, (dims, ((), ())), preferred_element_type=jnp.float32)


def iota(shape, dim):
    return lax.broadcasted_iota(jnp.int32, shape, dim)


def edges_kernel(grid_ref, _, first_ref, second_ref, found):
    channels, frames, height, columns = grid_ref.shape
    groups, wide = channels // GROUP, GROUP * height
    count = groups * frames
    even = lax.axis_index("tile") % 2 == 0
    ahead, behind = jnp.where(even, columns - 1, 0), jnp.where(even, 0, columns - 1)
    rows, lanes = iota((16, columns), 0), iota((16, columns), 1)
    pick = (((rows == 0) & (lanes == ahead)) | ((rows == 1) & (lanes == behind))).astype(jnp.bfloat16)
    for g in range(groups):
        for f in range(frames):
            at = g * frames + f
            cells = grid_ref[g * GROUP : (g + 1) * GROUP, f].reshape(wide, columns)
            both = dot(pick, cells, ((1,), (1,)))
            found[at : at + 1, :] = both[0:1]
            found[count + at : count + at + 1, :] = both[1:2]
    first_ref[...] = found[:count].astype(jnp.bfloat16)
    second_ref[...] = found[count:].astype(jnp.bfloat16)


def swaps(count, start):
    partner = {i: i for i in range(count)}
    for i in range(start, count - 1, 2):
        partner[i], partner[i + 1] = i + 1, i
    return sorted(partner.items())


def edge_columns(grid, after):
    channels, frames, height, _ = grid.shape
    shape = jax.ShapeDtypeStruct((channels // GROUP * frames, GROUP * height), jnp.bfloat16)
    return pl.pallas_call(
        edges_kernel,
        in_specs=[pl.BlockSpec(memory_space=pltpu.VMEM), pl.BlockSpec(memory_space=pl.ANY)],
        out_shape=(shape, shape),
        scratch_shapes=[pltpu.VMEM((2 * shape.shape[0], shape.shape[1]), jnp.float32)],
        compiler_params=params(8),
        cost_estimate=pl.CostEstimate(flops=2**28, bytes_accessed=2**21, transcendentals=0),
        name="edge_columns",
    )(grid, after)


def bands_kernel(height, taps_ref, band_ref, spread):
    _, inner, channels = taps_ref.shape
    wide = GROUP * height
    repeat = (iota((inner, wide), 0) == iota((inner, wide), 1) // height).astype(jnp.bfloat16)
    offset = iota((height, wide), 1) % height - iota((height, wide), 0)
    masks = [offset == row - 1 for row in range(3)]
    for tap in range(9):
        half = (taps_ref[tap].astype(jnp.float32) * 0.5).astype(jnp.bfloat16)
        spread[tap] = dot(half, repeat, ((0,), (0,)))

    for c in range(channels):
        out = c % GROUP * height
        for col in range(3):
            value = jnp.zeros((height, wide), jnp.float32)
            for row in range(3):
                value = jnp.where(masks[row], spread[3 * row + col, c : c + 1, :], value)
            band_ref[c // GROUP, out : out + height, col * wide : (col + 1) * wide] = value.astype(jnp.bfloat16)


def bands(conv_weight, height):
    taps = jnp.transpose(conv_weight, (0, 2, 1))
    channels = taps.shape[2]
    groups, wide = channels // GROUP, GROUP * height
    return pl.pallas_call(
        functools.partial(bands_kernel, height),
        out_shape=jax.ShapeDtypeStruct((groups, wide, 3 * wide), jnp.bfloat16),
        scratch_shapes=[pltpu.VMEM((9, channels, wide), jnp.float32)],
        compiler_params=params(8),
        cost_estimate=pl.CostEstimate(flops=2**28, bytes_accessed=2**23, transcendentals=0),
        name="bands",
    )(taps)


def inner_kernel(occupied_ref, bias_ref, grid_ref, band_ref, summed_ref, cells_ref, pick_ref, side_ref):
    channels, frames, height, columns = grid_ref.shape
    halves = columns // LANES
    wide = GROUP * height
    me, count = lax.axis_index("frame"), lax.axis_size("frame")
    slots = occupied_ref.shape[1] // count
    part = GROUP * slots
    rows, lanes = iota((part, wide), 0), iota((part, wide), 1)
    at_slot, at_side = rows % slots, iota((part, LANES), 0) % slots
    same_channel, at_row = lanes // height == rows // slots, lanes % height
    for d, step in enumerate(steps_of(count)):
        row, side = jnp.zeros((part, wide), jnp.int32), jnp.zeros((part, LANES), jnp.int32)
        for j in range(slots):
            block = occupied_ref[0, sent_to(me, step) * slots + j]
            row = jnp.where(at_slot == j, block // halves, row)
            side = jnp.where(at_side == j, block % halves, side)
        pick_ref[d * part : (d + 1) * part, :] = (same_channel & (at_row == row)).astype(jnp.bfloat16)
        side_ref[d * part : (d + 1) * part, :] = side

    tile_lanes = iota((wide, LANES), 1)
    is_first, is_last = tile_lanes == 0, tile_lanes == LANES - 1
    nothing = jnp.zeros((wide, LANES), jnp.float32)

    def shifted(g, f):
        cells = grid_ref[g * GROUP : (g + 1) * GROUP, f].reshape(wide, columns)
        full = cells.astype(jnp.float32)
        cells_ref[g, f] = full
        tiles = [full[:, side * LANES : (side + 1) * LANES] for side in range(halves)]
        right = [pltpu.roll(tile, 1, 1) for tile in tiles]
        left = [pltpu.roll(tile, LANES - 1, 1) for tile in tiles]
        before = [jnp.where(is_first, *pair) for pair in zip([nothing] + right[:-1], right)]
        after = [jnp.where(is_last, *pair) for pair in zip(left[1:] + [nothing], left)]
        before, after = (jnp.concatenate(parts, axis=1).astype(jnp.bfloat16) for parts in (before, after))
        return jnp.concatenate([before, cells, after], axis=0)

    items = [(g, f) for g in range(channels // GROUP) for f in range(frames)]
    ready = shifted(*items[0])
    for (g, f), following in zip(items, items[1:] + [None]):
        summed = dot(band_ref[g], ready)
        if following is not None:
            ready = shifted(*following)
        for out in range(GROUP):
            inside = slice(out * height, (out + 1) * height)
            summed_ref[g, f, inside, :] = summed[inside] + 0.5 * bias_ref[g * GROUP + out]


def inner(grid, band, conv_bias, occupied, parts):
    channels, frames, height, columns = grid.shape
    part = GROUP * (occupied.shape[1] // parts)
    smem, vmem = pl.BlockSpec(memory_space=pltpu.SMEM), pl.BlockSpec(memory_space=pltpu.VMEM)
    wide = jax.ShapeDtypeStruct((channels // GROUP, frames, GROUP * height, columns), jnp.float32)
    return pl.pallas_call(
        inner_kernel,
        in_specs=[smem, smem, vmem, vmem],
        out_shape=(
            wide,
            wide,
            jax.ShapeDtypeStruct((parts * part, GROUP * height), jnp.bfloat16),
            jax.ShapeDtypeStruct((parts * part, LANES), jnp.int32),
        ),
        compiler_params=params(8),
        cost_estimate=pl.CostEstimate(flops=2**31, bytes_accessed=2**23, transcendentals=0),
        name="inner",
    )(occupied, conv_bias, grid, band)


def steps_of(count, core_first=False):
    mixed = [(4, 2), (2, 4), (5, 3), (3, 5)] if count >= 8 else []
    seen = {0, 1} | {a for a, _ in mixed}
    across = mixed + [(d, d) for d in range(count) if d not in seen]
    return [(0, 0), (1, 1)] + across if core_first else [(0, 0)] + across + [(1, 1)]


def sent_to(me, step):
    return me ^ jnp.where(me % 2 == 0, step[0], step[1])


def got_from(me, step):
    return sent_to(me, step) if step[0] % 2 == 0 else sent_to(me, step[::-1])


def finish_kernel(band_ref, summed_ref, cells_ref, pick_ref, side_ref, first_ref, second_ref, hidden_ref, *message_refs):
    channels, frames, height, columns = hidden_ref.shape
    halves = columns // LANES
    wide = GROUP * height
    part = pick_ref.shape[0] // len(message_refs)
    tile, tiles = lax.axis_index("tile"), lax.axis_size("tile")
    even = tile % 2 == 0
    first, second = first_ref[...].astype(jnp.float32), second_ref[...].astype(jnp.float32)
    left = jnp.where(tile > 0, jnp.where(even, second, first), 0.0)
    right = jnp.where(tile < tiles - 1, jnp.where(even, first, second), 0.0)
    rim = 16
    rim_rows = iota((rim, wide), 0)
    blank = jnp.zeros((LANES - rim, wide), jnp.bfloat16)

    def edge_terms(g):
        before, after = [], []
        for f in range(frames):
            at = slice(g * frames + f, g * frames + f + 1)
            before += [jnp.where(rim_rows == 0, left[at], 0.0).astype(jnp.bfloat16), blank]
            after += [blank, jnp.where(rim_rows == rim - 1, right[at], 0.0).astype(jnp.bfloat16)]
        return (
            dot(band_ref[g, :, :wide], jnp.concatenate(before, axis=0), ((1,), (1,))),
            dot(band_ref[g, :, 2 * wide :], jnp.concatenate(after, axis=0), ((1,), (1,))),
        )

    def activate(g, at_left, at_right):
        for f in range(frames):
            across = slice(f * LANES, (f + 1) * LANES)
            for out in range(GROUP):
                c = g * GROUP + out
                part = slice(out * height, (out + 1) * height)
                half = summed_ref[g, f, part, :]
                tiles = [half[:, side * LANES : (side + 1) * LANES] for side in range(halves)]
                tiles[0] += at_left[part, across]
                tiles[-1] += at_right[part, across]
                half = jnp.concatenate(tiles, axis=1)
                hidden = cells_ref[g, f, part, :] + (half + half * jnp.tanh(half))
                hidden_ref[c, f] = hidden.astype(jnp.bfloat16)

    def pick(g):
        return [
            dot(pick_ref[...], hidden_ref[g * GROUP : (g + 1) * GROUP, f].reshape(wide, columns))
            for f in range(frames)
        ]

    def send(g, picks):
        for f, picked in enumerate(picks):
            chosen = picked[:, :LANES]
            for side in range(1, halves):
                chosen = jnp.where(side_ref[...] == side, picked[:, side * LANES : (side + 1) * LANES], chosen)
            chosen = chosen.astype(jnp.bfloat16)
            for d, message_ref in enumerate(message_refs):
                message_ref[f, g * part : (g + 1) * part, :] = chosen[d * part : (d + 1) * part]

    groups = channels // GROUP
    terms = edge_terms(0)
    for g in range(groups):
        current = terms
        picks = pick(g - 1) if g > 0 else None
        terms = edge_terms(g + 1) if g + 1 < groups else None
        activate(g, *current)
        if picks is not None:
            send(g - 1, picks)
    send(groups - 1, pick(groups - 1))


def finish(grid, band, summed, cells, pick, side, first, second, parts):
    channels, frames, _, _ = grid.shape
    slots = pick.shape[0] // (GROUP * parts)
    vmem = pl.BlockSpec(memory_space=pltpu.VMEM)
    return pl.pallas_call(
        finish_kernel,
        in_specs=[vmem] * 7,
        out_shape=[jax.ShapeDtypeStruct(grid.shape, jnp.bfloat16)]
        + [jax.ShapeDtypeStruct((frames, channels * slots, LANES), jnp.bfloat16)] * parts,
        compiler_params=params(8),
        cost_estimate=pl.CostEstimate(flops=2**30, bytes_accessed=2**23, transcendentals=2**20),
        name="finish",
    )(band, summed, cells, pick, side, first, second)


def tables_kernel(depth_ref, point_ref, _, table_ref, mix_ref):
    layers, channels, _ = point_ref.shape
    taps = depth_ref.shape[0]
    tall = mix_ref.shape[1]
    slots = tall // channels
    same_channel = iota((tall, channels), 0) // slots == iota((tall, channels), 1)
    up = same_channel.astype(jnp.bfloat16)
    across = (iota((channels, tall), 1) // slots == iota((channels, tall), 0)).astype(jnp.bfloat16)
    same_slot = iota((tall, tall), 0) % slots == iota((tall, tall), 1) % slots
    for layer in range(layers):
        for tap in range(taps):
            row = 0.5 * depth_ref[tap, layer : layer + 1, :]
            column = jnp.sum(jnp.where(same_channel, row, 0.0), axis=1, keepdims=True)
            table_ref[layer * taps + tap] = jnp.broadcast_to(column, table_ref.shape[1:])
        spread = dot(dot(up, point_ref[layer]).astype(jnp.bfloat16), across)
        mix_ref[layer] = jnp.where(same_slot, spread, 0.0).astype(jnp.bfloat16)


def tables(depth_kernel, point_weight, slots, after):
    layers, taps, channels = depth_kernel.shape
    vmem = pl.BlockSpec(memory_space=pltpu.VMEM)
    return pl.pallas_call(
        tables_kernel,
        in_specs=[vmem, vmem, pl.BlockSpec(memory_space=pl.ANY)],
        out_shape=(
            jax.ShapeDtypeStruct((layers * taps, channels * slots, LANES), jnp.float32),
            jax.ShapeDtypeStruct((layers, channels * slots, channels * slots), jnp.bfloat16),
        ),
        compiler_params=params(8),
        cost_estimate=pl.CostEstimate(flops=2**27, bytes_accessed=2**22, transcendentals=0),
        name="tables",
    )(jnp.transpose(depth_kernel, (1, 0, 2)), point_weight, after)


def temporal_kernel(sources, depth_ref, mix_ref, *refs):
    message_refs, out_refs = refs[:sources], refs[sources : 2 * sources]
    state, squashed, final = refs[2 * sources :]
    me = lax.axis_index("frame")
    local, tall, lanes = message_refs[0].shape
    frames = sources * local
    layers = mix_ref.shape[0]
    taps = depth_ref.shape[0] // layers
    quads, _, width = squashed.shape
    quad = width // lanes
    for step, message_ref in zip(steps_of(sources), message_refs):
        for f in range(local):
            state[got_from(me, step) * local + f] = message_ref[f].astype(jnp.float32)
    height = 32

    def blend(layer, q):
        spacing = 2**layer
        inside = range(q * quad, (q + 1) * quad)
        for top in range(0, tall, height):
            part = slice(top, top + height)
            scale = [depth_ref[layer * taps + tap, part] for tap in range(taps)]
            needed = {f - tap * spacing for f in inside for tap in range(taps)}
            series = {f: state[f, part] for f in sorted(needed) if f >= 0}
            for f in inside:
                half = scale[0] * series[f]
                for tap in range(1, taps):
                    if f >= tap * spacing:
                        half += scale[tap] * series[f - tap * spacing]
                across = slice((f - q * quad) * lanes, (f - q * quad + 1) * lanes)
                squashed[q, part, across] = (half + half * jnp.tanh(half)).astype(jnp.bfloat16)

    def update(layer, q, mixed):
        for f in range(q * quad, (q + 1) * quad):
            after = state[f] + mixed[:, (f - q * quad) * lanes : (f - q * quad + 1) * lanes]
            if layer + 1 < layers:
                state[f] = after
            else:
                final[f] = after.astype(jnp.bfloat16)

    waiting = None
    for layer in range(layers):
        for q in reversed(range(quads)):
            reads = {(f - tap * 2**layer) // quad for f in range(q * quad, (q + 1) * quad) for tap in range(taps)}
            late = waiting is not None and waiting[1] not in reads
            if waiting is not None and not late:
                update(*waiting)
            blend(layer, q)
            if late:
                update(*waiting)
            waiting = layer, q, dot(mix_ref[layer], squashed[q])
    update(*waiting)
    for step, out_ref in zip(steps_of(sources, True), out_refs):
        for f in range(local):
            out_ref[f] = final[sent_to(me, step) * local + f]


def temporal(messages, depth, mix):
    sources = len(messages)
    local, tall, lanes = messages[0].shape
    vmem = pl.BlockSpec(memory_space=pltpu.VMEM)
    return pl.pallas_call(
        functools.partial(temporal_kernel, sources),
        in_specs=[vmem, vmem] + [vmem] * sources,
        out_shape=[jax.ShapeDtypeStruct(messages[0].shape, jnp.bfloat16)] * sources,
        scratch_shapes=[
            pltpu.VMEM((sources * local, tall, lanes), jnp.float32),
            pltpu.VMEM((sources * local // 4, tall, 4 * lanes), jnp.bfloat16),
            pltpu.VMEM((sources * local, tall, lanes), jnp.bfloat16),
        ],
        compiler_params=params(12),
        cost_estimate=pl.CostEstimate(flops=2**30, bytes_accessed=2**21, transcendentals=2**21),
        name="temporal",
    )(depth, mix, *messages)


def plan_kernel(sources, occupied_ref, counts_ref, _, put_ref, cover_ref):
    me = lax.axis_index("frame")
    halves, wide, tall = put_ref.shape
    part = tall // sources
    slots = part // GROUP
    height = wide // GROUP
    rows, lanes = iota((part, wide), 0), iota((part, wide), 1)
    same_channel, at_slot, at_row = lanes // height == rows // slots, rows % slots, lanes % height
    for side in range(halves):
        hits = []
        for step in steps_of(sources, True):
            row = jnp.full((part, wide), -1, jnp.int32)
            for j in range(slots):
                slot = got_from(me, step) * slots + j
                block = occupied_ref[0, slot]
                used = (slot < counts_ref[0]) & (block % halves == side)
                row = jnp.where(at_slot == j, jnp.where(used, block // halves, -1), row)
            hits.append((same_channel & (at_row == row)).astype(jnp.float32))
        put = jnp.transpose(jnp.concatenate(hits, axis=0)).astype(jnp.bfloat16)
        put_ref[side] = put
        cover_ref[side] = dot(put, jnp.ones((tall, LANES), jnp.bfloat16))


def plan(occupied, counts, wide, halves, sources, after):
    smem = pl.BlockSpec(memory_space=pltpu.SMEM)
    return pl.pallas_call(
        functools.partial(plan_kernel, sources),
        in_specs=[smem, smem, pl.BlockSpec(memory_space=pl.ANY)],
        out_shape=(
            jax.ShapeDtypeStruct((halves, wide, GROUP * occupied.shape[1]), jnp.bfloat16),
            jax.ShapeDtypeStruct((halves, wide, LANES), jnp.float32),
        ),
        compiler_params=params(8),
        cost_estimate=pl.CostEstimate(flops=2**27, bytes_accessed=2**22, transcendentals=0),
        name="plan",
    )(occupied, counts, after)


def place_kernel(sources, put_ref, cover_ref, hidden_ref, *refs):
    message_refs, (out_hbm, out_ref, sems) = refs[:sources], refs[sources:]
    channels, frames, height, columns = hidden_ref.shape
    halves = columns // LANES
    wide = GROUP * height
    part = put_ref.shape[2] // sources

    def group_copy(g):
        cells = pl.ds(g * GROUP, GROUP)
        return pltpu.make_async_copy(out_ref.at[cells], out_hbm.at[cells], sems.at[g])

    def spread(g):
        rows = slice(g * part, (g + 1) * part)
        updated = jnp.concatenate(
            [jnp.concatenate([ref[f, rows, :] for f in range(frames)], axis=1) for ref in message_refs], axis=0
        )
        return [dot(put_ref[side], updated) for side in range(halves)]

    def merge(g, spreads):
        base = g * GROUP
        for side in range(halves):
            across = slice(side * LANES, (side + 1) * LANES)
            for f in range(frames):
                cells = hidden_ref[base : base + GROUP, f, :, across].reshape(wide, LANES).astype(jnp.float32)
                merged = jnp.where(cover_ref[side] > 0.5, spreads[side][:, f * LANES : (f + 1) * LANES], cells)
                out_ref[base : base + GROUP, f, :, across] = merged.astype(jnp.bfloat16).reshape(GROUP, height, LANES)
        group_copy(g).start()

    groups = channels // GROUP
    following = spread(0)
    for g in range(groups):
        current = following
        following = spread(g + 1) if g + 1 < groups else None
        merge(g, current)
    for g in range(groups):
        group_copy(g).wait()


def place(hidden, messages, put, cover):
    channels = hidden.shape[0]
    sources = len(messages)
    vmem, anywhere = pl.BlockSpec(memory_space=pltpu.VMEM), pl.BlockSpec(memory_space=pl.ANY)
    return pl.pallas_call(
        functools.partial(place_kernel, sources),
        in_specs=[vmem, vmem, vmem] + [vmem] * sources,
        out_specs=anywhere,
        out_shape=jax.ShapeDtypeStruct(hidden.shape, jnp.bfloat16),
        scratch_shapes=[
            pltpu.VMEM(hidden.shape, jnp.bfloat16),
            pltpu.SemaphoreType.DMA((channels // GROUP,)),
        ],
        compiler_params=params(8),
        cost_estimate=pl.CostEstimate(flops=2**28, bytes_accessed=2**22, transcendentals=0),
        name="place",
    )(put, cover, hidden, *messages)


def exchange(arrays, core_first):
    count = len(arrays)
    return [
        array if step == (0, 0) else lax.ppermute(array, "frame", [(i, i ^ step[i % 2]) for i in range(count)])
        for array, step in zip(arrays, steps_of(count, core_first))
    ]


def on_device(grid, conv_weight, conv_bias, depth_kernel, point_weight, occupied, counts):
    channels, frames, height, columns = grid.shape
    tiles, parts = lax.axis_size("tile"), lax.axis_size("frame")
    slots = occupied.shape[1] // parts
    band = bands(conv_weight, height)
    first, second = edge_columns(grid, band)
    first = lax.ppermute(first, "tile", swaps(tiles, 0))
    second = lax.ppermute(second, "tile", swaps(tiles, 1))
    inside = inner(grid, band, conv_bias, occupied, parts)
    hidden, *messages = finish(grid, band, *inside, first, second, parts)
    depth, mix = tables(depth_kernel, point_weight, slots, messages[0])
    updated = temporal(exchange(messages, False), depth, mix)
    put, cover = plan(occupied, counts, GROUP * height, columns // LANES, parts, updated[0])
    return place(hidden, exchange(updated, True), put, cover)


def solution(mesh):
    placed = (P(None, "frame", None, "tile"), P(), P(), P(), P(), P("tile", None), P("tile"))
    return jax.shard_map(
        on_device,
        mesh=mesh,
        in_specs=placed,
        out_specs=P(None, "frame", None, "tile"),
        check_vma=False,
    )
```

```python
import functools

import jax
import jax.numpy as jnp
from jax import lax
from jax.experimental import pallas as pl
from jax.experimental.pallas import tpu as pltpu
from jax.sharding import PartitionSpec as P

GROUP = 8
LANES = 128
MIB = 2**20


def params(mib):
    return pltpu.CompilerParams(vmem_limit_bytes=mib * MIB)


def whole(shape):
    return pl.BlockSpec(shape, lambda *_: (0,) * len(shape))


def dot(a, b, dims=((1,), (0,))):
    return lax.dot_general(a, b, (dims, ((), ())), preferred_element_type=jnp.float32)


def quotient(value, size):
    return value >> (size.bit_length() - 1) if size & (size - 1) == 0 else value // size


def remainder(value, size):
    return value & (size - 1) if size & (size - 1) == 0 else value % size


def iota(shape, dim):
    return lax.broadcasted_iota(jnp.int32, shape, dim)


def edges_kernel(grid_ref, _, first_ref, second_ref, found):
    channels, frames, height, columns = grid_ref.shape
    groups, wide = channels // GROUP, GROUP * height
    count = groups * frames
    even = lax.axis_index("tile") % 2 == 0
    ahead, behind = jnp.where(even, columns - 1, 0), jnp.where(even, 0, columns - 1)
    rows, lanes = iota((16, columns), 0), iota((16, columns), 1)
    pick = (((rows == 0) & (lanes == ahead)) | ((rows == 1) & (lanes == behind))).astype(jnp.bfloat16)
    for g in range(groups):
        for f in range(frames):
            at = g * frames + f
            cells = grid_ref[g * GROUP : (g + 1) * GROUP, f].reshape(wide, columns)
            both = dot(pick, cells, ((1,), (1,)))
            found[at : at + 1, :] = both[0:1]
            found[count + at : count + at + 1, :] = both[1:2]
    first_ref[...] = found[:count].astype(jnp.bfloat16)
    second_ref[...] = found[count:].astype(jnp.bfloat16)


def swaps(count, start):
    partner = {i: i for i in range(count)}
    for i in range(start, count - 1, 2):
        partner[i], partner[i + 1] = i + 1, i
    return sorted(partner.items())


def edge_columns(grid, after):
    channels, frames, height, _ = grid.shape
    shape = jax.ShapeDtypeStruct((channels // GROUP * frames, GROUP * height), jnp.bfloat16)
    return pl.pallas_call(
        edges_kernel,
        in_specs=[pl.BlockSpec(memory_space=pltpu.VMEM), pl.BlockSpec(memory_space=pl.ANY)],
        out_shape=(shape, shape),
        scratch_shapes=[pltpu.VMEM((2 * shape.shape[0], shape.shape[1]), jnp.float32)],
        compiler_params=params(8),
        cost_estimate=pl.CostEstimate(flops=2**28, bytes_accessed=2**21, transcendentals=0),
        name="edge_columns",
    )(grid, after)


def bands_kernel(height, taps_ref, band_ref, spread):
    _, inner, channels = taps_ref.shape
    wide = GROUP * height
    repeat = (iota((inner, wide), 0) == iota((inner, wide), 1) // height).astype(jnp.bfloat16)
    for tap in range(9):
        half = (taps_ref[tap].astype(jnp.float32) * 0.5).astype(jnp.bfloat16)
        spread[tap] = dot(half, repeat, ((0,), (0,)))
    strip = 16
    offset = remainder(iota((height, wide), 1), height) - iota((height, wide), 0)
    offset = offset.astype(jnp.float32).astype(jnp.bfloat16)
    masks = [
        [offset[top : top + strip] == jnp.bfloat16(row - 1) for row in range(3)] for top in range(0, height, strip)
    ]
    for c in range(channels):
        for col in range(3):
            rows = [
                jnp.broadcast_to(spread[3 * row + col, c : c + 1, :], (strip, wide)).astype(jnp.bfloat16)
                for row in range(3)
            ]
            for at, mask in enumerate(masks):
                value = jnp.zeros((strip, wide), jnp.bfloat16)
                for row in range(3):
                    value = jnp.where(mask[row], rows[row], value)
                top = c % GROUP * height + at * strip
                band_ref[c // GROUP, top : top + strip, col * wide : (col + 1) * wide] = value


def bands(conv_weight, height):
    taps = jnp.transpose(conv_weight, (0, 2, 1))
    channels = taps.shape[2]
    groups, wide = channels // GROUP, GROUP * height
    return pl.pallas_call(
        functools.partial(bands_kernel, height),
        out_shape=jax.ShapeDtypeStruct((groups, wide, 3 * wide), jnp.bfloat16),
        scratch_shapes=[pltpu.VMEM((9, channels, wide), jnp.float32)],
        compiler_params=params(8),
        cost_estimate=pl.CostEstimate(flops=2**28, bytes_accessed=2**23, transcendentals=0),
        name="bands",
    )(taps)


def inner_kernel(occupied_ref, bias_ref, grid_ref, band_ref, summed_ref, cells_ref, pick_ref, side_ref):
    channels, frames, height, columns = grid_ref.shape
    halves = columns // LANES
    wide = GROUP * height
    me, count = lax.axis_index("frame"), lax.axis_size("frame")
    slots = occupied_ref.shape[1] // count
    part = GROUP * slots
    rows, lanes = iota((part, wide), 0), iota((part, wide), 1)
    at_slot, at_side = remainder(rows, slots), remainder(iota((part, LANES), 0), slots)
    same_channel, at_row = quotient(lanes, height) == quotient(rows, slots), remainder(lanes, height)
    for d, step in enumerate(steps_of(count)):
        row, side = jnp.zeros((part, wide), jnp.int32), jnp.zeros((part, LANES), jnp.int32)
        first = sent_to(me, step) * slots
        for j in range(slots):
            block = occupied_ref[0, first + j]
            row = jnp.where(at_slot == j, quotient(block, halves), row)
            side = jnp.where(at_side == j, remainder(block, halves), side)
        pick_ref[d * part : (d + 1) * part, :] = (same_channel & (at_row == row)).astype(jnp.bfloat16)
        side_ref[d * part : (d + 1) * part, :] = side

    tile_lanes = iota((wide, LANES), 1)
    is_first, is_last = tile_lanes == 0, tile_lanes == LANES - 1
    nothing = jnp.zeros((wide, LANES), jnp.bfloat16)

    def shifted(g, f):
        cells = grid_ref[g * GROUP : (g + 1) * GROUP, f].reshape(wide, columns)
        tiles = [cells[:, side * LANES : (side + 1) * LANES] for side in range(halves)]
        right = [pltpu.roll(tile, 1, 1) for tile in tiles]
        left = [pltpu.roll(tile, LANES - 1, 1) for tile in tiles]
        before = [jnp.where(is_first, *pair) for pair in zip([nothing] + right[:-1], right)]
        after = [jnp.where(is_last, *pair) for pair in zip(left[1:] + [nothing], left)]
        return jnp.concatenate([jnp.concatenate(before, axis=1), cells, jnp.concatenate(after, axis=1)], axis=0)

    items = [(g, f) for g in range(channels // GROUP) for f in range(frames)]
    ready = shifted(*items[0])
    for (g, f), following in zip(items, items[1:] + [None]):
        summed = dot(band_ref[g], ready)
        if following is not None:
            ready = shifted(*following)
        for out in range(GROUP):
            inside = slice(out * height, (out + 1) * height)
            summed_ref[g, f, inside, :] = summed[inside] + 0.5 * bias_ref[g * GROUP + out]
            cells_ref[g, f, inside, :] = grid_ref[g * GROUP + out, f].astype(jnp.float32)


def inner(grid, band, conv_bias, occupied, parts):
    channels, frames, height, columns = grid.shape
    part = GROUP * (occupied.shape[1] // parts)
    smem, vmem = pl.BlockSpec(memory_space=pltpu.SMEM), pl.BlockSpec(memory_space=pltpu.VMEM)
    wide = jax.ShapeDtypeStruct((channels // GROUP, frames, GROUP * height, columns), jnp.float32)
    return pl.pallas_call(
        inner_kernel,
        in_specs=[smem, smem, vmem, vmem],
        out_shape=(
            wide,
            wide,
            jax.ShapeDtypeStruct((parts * part, GROUP * height), jnp.bfloat16),
            jax.ShapeDtypeStruct((parts * part, LANES), jnp.int32),
        ),
        compiler_params=params(8),
        cost_estimate=pl.CostEstimate(flops=2**31, bytes_accessed=2**23, transcendentals=0),
        name="inner",
    )(occupied, conv_bias, grid, band)


def steps_of(count, core_first=False):
    mixed = [(4, 2), (2, 4), (5, 3), (3, 5)] if count >= 8 else []
    seen = {0, 1} | {a for a, _ in mixed}
    across = mixed + [(d, d) for d in range(count) if d not in seen]
    return [(0, 0), (1, 1)] + across if core_first else [(0, 0)] + across + [(1, 1)]


def sent_to(me, step):
    return me ^ jnp.where(remainder(me, 2) == 0, step[0], step[1])


def got_from(me, step):
    return sent_to(me, step) if step[0] % 2 == 0 else sent_to(me, step[::-1])


def finish_kernel(band_ref, summed_ref, cells_ref, pick_ref, side_ref, first_ref, second_ref, hidden_ref, *message_refs):
    channels, frames, height, columns = hidden_ref.shape
    halves = columns // LANES
    wide = GROUP * height
    part = pick_ref.shape[0] // len(message_refs)
    tile, tiles = lax.axis_index("tile"), lax.axis_size("tile")
    even = tile % 2 == 0
    first, second = first_ref[...].astype(jnp.float32), second_ref[...].astype(jnp.float32)
    left = jnp.where(tile > 0, jnp.where(even, second, first), 0.0)
    right = jnp.where(tile < tiles - 1, jnp.where(even, first, second), 0.0)
    rim = 16
    rim_rows = iota((rim, wide), 0)
    blank = jnp.zeros((LANES - rim, wide), jnp.bfloat16)

    def edge_terms(g):
        before, after = [], []
        for f in range(frames):
            at = slice(g * frames + f, g * frames + f + 1)
            before += [jnp.where(rim_rows == 0, left[at], 0.0).astype(jnp.bfloat16), blank]
            after += [blank, jnp.where(rim_rows == rim - 1, right[at], 0.0).astype(jnp.bfloat16)]
        return (
            dot(band_ref[g, :, :wide], jnp.concatenate(before, axis=0), ((1,), (1,))),
            dot(band_ref[g, :, 2 * wide :], jnp.concatenate(after, axis=0), ((1,), (1,))),
        )

    def activate(g, at_left, at_right):
        for f in range(frames):
            across = slice(f * LANES, (f + 1) * LANES)
            for out in range(GROUP):
                c = g * GROUP + out
                part = slice(out * height, (out + 1) * height)
                half = summed_ref[g, f, part, :]
                tiles = [half[:, side * LANES : (side + 1) * LANES] for side in range(halves)]
                tiles[0] += at_left[part, across]
                tiles[-1] += at_right[part, across]
                half = jnp.concatenate(tiles, axis=1)
                hidden = cells_ref[g, f, part, :] + (half + half * jnp.tanh(half))
                hidden_ref[c, f] = hidden.astype(jnp.bfloat16)

    def pick(g):
        return [
            dot(pick_ref[...], hidden_ref[g * GROUP : (g + 1) * GROUP, f].reshape(wide, columns))
            for f in range(frames)
        ]

    def send(g, picks):
        for f, picked in enumerate(picks):
            chosen = picked[:, :LANES]
            for side in range(1, halves):
                chosen = jnp.where(side_ref[...] == side, picked[:, side * LANES : (side + 1) * LANES], chosen)
            chosen = chosen.astype(jnp.bfloat16)
            for d, message_ref in enumerate(message_refs):
                message_ref[f, g * part : (g + 1) * part, :] = chosen[d * part : (d + 1) * part]

    groups = channels // GROUP
    terms = edge_terms(0)
    for g in range(groups):
        current = terms
        picks = pick(g - 1) if g > 0 else None
        terms = edge_terms(g + 1) if g + 1 < groups else None
        activate(g, *current)
        if picks is not None:
            send(g - 1, picks)
    send(groups - 1, pick(groups - 1))


def finish(grid, band, summed, cells, pick, side, first, second, parts):
    channels, frames, _, _ = grid.shape
    slots = pick.shape[0] // (GROUP * parts)
    vmem = pl.BlockSpec(memory_space=pltpu.VMEM)
    return pl.pallas_call(
        finish_kernel,
        in_specs=[vmem] * 7,
        out_shape=[jax.ShapeDtypeStruct(grid.shape, jnp.bfloat16)]
        + [jax.ShapeDtypeStruct((frames, channels * slots, LANES), jnp.bfloat16)] * parts,
        compiler_params=params(8),
        cost_estimate=pl.CostEstimate(flops=2**30, bytes_accessed=2**23, transcendentals=2**20),
        name="finish",
    )(band, summed, cells, pick, side, first, second)


def tables_kernel(depth_ref, point_ref, _, table_ref, mix_ref):
    layers, channels, _ = point_ref.shape
    taps = depth_ref.shape[0]
    tall = mix_ref.shape[1]
    slots = tall // channels
    same_channel = iota((tall, channels), 0) // slots == iota((tall, channels), 1)
    up = same_channel.astype(jnp.bfloat16)
    across = (iota((channels, tall), 1) // slots == iota((channels, tall), 0)).astype(jnp.bfloat16)
    same_slot = iota((tall, tall), 0) % slots == iota((tall, tall), 1) % slots
    for layer in range(layers):
        for tap in range(taps):
            row = 0.5 * depth_ref[tap, layer : layer + 1, :]
            column = jnp.sum(jnp.where(same_channel, row, 0.0), axis=1, keepdims=True)
            table_ref[layer * taps + tap] = jnp.broadcast_to(column, table_ref.shape[1:])
        spread = dot(dot(up, point_ref[layer]).astype(jnp.bfloat16), across)
        mix_ref[layer] = jnp.where(same_slot, spread, 0.0).astype(jnp.bfloat16)


def tables(depth_kernel, point_weight, slots, after):
    layers, taps, channels = depth_kernel.shape
    vmem = pl.BlockSpec(memory_space=pltpu.VMEM)
    return pl.pallas_call(
        tables_kernel,
        in_specs=[vmem, vmem, pl.BlockSpec(memory_space=pl.ANY)],
        out_shape=(
            jax.ShapeDtypeStruct((layers * taps, channels * slots, LANES), jnp.float32),
            jax.ShapeDtypeStruct((layers, channels * slots, channels * slots), jnp.bfloat16),
        ),
        compiler_params=params(8),
        cost_estimate=pl.CostEstimate(flops=2**27, bytes_accessed=2**22, transcendentals=0),
        name="tables",
    )(jnp.transpose(depth_kernel, (1, 0, 2)), point_weight, after)


def temporal_kernel(sources, depth_ref, mix_ref, *refs):
    message_refs, out_refs = refs[:sources], refs[sources : 2 * sources]
    state, squashed, final = refs[2 * sources :]
    me = lax.axis_index("frame")
    local, tall, lanes = message_refs[0].shape
    frames = sources * local
    layers = mix_ref.shape[0]
    taps = depth_ref.shape[0] // layers
    quads, _, width = squashed.shape
    quad = width // lanes
    for step, message_ref in zip(steps_of(sources), message_refs):
        for f in range(local):
            state[got_from(me, step) * local + f] = message_ref[f].astype(jnp.float32)
    height = 32

    def blend(layer, q):
        spacing = 2**layer
        inside = range(q * quad, (q + 1) * quad)
        for top in range(0, tall, height):
            part = slice(top, top + height)
            scale = [depth_ref[layer * taps + tap, part] for tap in range(taps)]
            needed = {f - tap * spacing for f in inside for tap in range(taps)}
            series = {f: state[f, part] for f in sorted(needed) if f >= 0}
            for f in inside:
                half = scale[0] * series[f]
                for tap in range(1, taps):
                    if f >= tap * spacing:
                        half += scale[tap] * series[f - tap * spacing]
                across = slice((f - q * quad) * lanes, (f - q * quad + 1) * lanes)
                squashed[q, part, across] = (half + half * jnp.tanh(half)).astype(jnp.bfloat16)

    def update(layer, q, mixed):
        for f in range(q * quad, (q + 1) * quad):
            after = state[f] + mixed[:, (f - q * quad) * lanes : (f - q * quad + 1) * lanes]
            if layer + 1 < layers:
                state[f] = after
            else:
                final[f] = after.astype(jnp.bfloat16)

    waiting = None
    for layer in range(layers):
        for q in reversed(range(quads)):
            reads = {(f - tap * 2**layer) // quad for f in range(q * quad, (q + 1) * quad) for tap in range(taps)}
            late = waiting is not None and waiting[1] not in reads
            if waiting is not None and not late:
                update(*waiting)
            blend(layer, q)
            if late:
                update(*waiting)
            waiting = layer, q, dot(mix_ref[layer], squashed[q])
    update(*waiting)
    for step, out_ref in zip(steps_of(sources, True), out_refs):
        for f in range(local):
            out_ref[f] = final[sent_to(me, step) * local + f]


def temporal(messages, depth, mix):
    sources = len(messages)
    local, tall, lanes = messages[0].shape
    vmem = pl.BlockSpec(memory_space=pltpu.VMEM)
    return pl.pallas_call(
        functools.partial(temporal_kernel, sources),
        in_specs=[vmem, vmem] + [vmem] * sources,
        out_shape=[jax.ShapeDtypeStruct(messages[0].shape, jnp.bfloat16)] * sources,
        scratch_shapes=[
            pltpu.VMEM((sources * local, tall, lanes), jnp.float32),
            pltpu.VMEM((sources * local // 4, tall, 4 * lanes), jnp.bfloat16),
            pltpu.VMEM((sources * local, tall, lanes), jnp.bfloat16),
        ],
        compiler_params=params(12),
        cost_estimate=pl.CostEstimate(flops=2**30, bytes_accessed=2**21, transcendentals=2**21),
        name="temporal",
    )(depth, mix, *messages)


def plan_kernel(sources, occupied_ref, counts_ref, _, put_ref, cover_ref):
    me = lax.axis_index("frame")
    halves, wide, tall = put_ref.shape
    part = tall // sources
    slots = part // GROUP
    height = wide // GROUP
    rows, lanes = iota((part, wide), 0), iota((part, wide), 1)
    same_channel, at_slot, at_row = lanes // height == rows // slots, rows % slots, lanes % height
    for side in range(halves):
        hits = []
        for step in steps_of(sources, True):
            row = jnp.full((part, wide), -1, jnp.int32)
            for j in range(slots):
                slot = got_from(me, step) * slots + j
                block = occupied_ref[0, slot]
                used = (slot < counts_ref[0]) & (block % halves == side)
                row = jnp.where(at_slot == j, jnp.where(used, block // halves, -1), row)
            hits.append((same_channel & (at_row == row)).astype(jnp.float32))
        put = jnp.transpose(jnp.concatenate(hits, axis=0)).astype(jnp.bfloat16)
        put_ref[side] = put
        cover_ref[side] = dot(put, jnp.ones((tall, LANES), jnp.bfloat16))


def plan(occupied, counts, wide, halves, sources, after):
    smem = pl.BlockSpec(memory_space=pltpu.SMEM)
    return pl.pallas_call(
        functools.partial(plan_kernel, sources),
        in_specs=[smem, smem, pl.BlockSpec(memory_space=pl.ANY)],
        out_shape=(
            jax.ShapeDtypeStruct((halves, wide, GROUP * occupied.shape[1]), jnp.bfloat16),
            jax.ShapeDtypeStruct((halves, wide, LANES), jnp.float32),
        ),
        compiler_params=params(8),
        cost_estimate=pl.CostEstimate(flops=2**27, bytes_accessed=2**22, transcendentals=0),
        name="plan",
    )(occupied, counts, after)


def place_kernel(sources, put_ref, cover_ref, hidden_ref, *refs):
    message_refs, (out_hbm, out_ref, sems) = refs[:sources], refs[sources:]
    channels, frames, height, columns = hidden_ref.shape
    halves = columns // LANES
    wide = GROUP * height
    part = put_ref.shape[2] // sources

    def group_copy(g):
        cells = pl.ds(g * GROUP, GROUP)
        return pltpu.make_async_copy(out_ref.at[cells], out_hbm.at[cells], sems.at[g])

    def spread(g):
        rows = slice(g * part, (g + 1) * part)
        updated = jnp.concatenate(
            [jnp.concatenate([ref[f, rows, :] for f in range(frames)], axis=1) for ref in message_refs], axis=0
        )
        return [dot(put_ref[side], updated) for side in range(halves)]

    def merge(g, spreads):
        base = g * GROUP
        for side in range(halves):
            across = slice(side * LANES, (side + 1) * LANES)
            for f in range(frames):
                cells = hidden_ref[base : base + GROUP, f, :, across].reshape(wide, LANES).astype(jnp.float32)
                merged = jnp.where(cover_ref[side] > 0.5, spreads[side][:, f * LANES : (f + 1) * LANES], cells)
                out_ref[base : base + GROUP, f, :, across] = merged.astype(jnp.bfloat16).reshape(GROUP, height, LANES)
        group_copy(g).start()

    groups = channels // GROUP
    following = spread(0)
    for g in range(groups):
        current = following
        following = spread(g + 1) if g + 1 < groups else None
        merge(g, current)
    for g in range(groups):
        group_copy(g).wait()


def place(hidden, messages, put, cover):
    channels = hidden.shape[0]
    sources = len(messages)
    vmem, anywhere = pl.BlockSpec(memory_space=pltpu.VMEM), pl.BlockSpec(memory_space=pl.ANY)
    return pl.pallas_call(
        functools.partial(place_kernel, sources),
        in_specs=[vmem, vmem, vmem] + [vmem] * sources,
        out_specs=anywhere,
        out_shape=jax.ShapeDtypeStruct(hidden.shape, jnp.bfloat16),
        scratch_shapes=[
            pltpu.VMEM(hidden.shape, jnp.bfloat16),
            pltpu.SemaphoreType.DMA((channels // GROUP,)),
        ],
        compiler_params=params(8),
        cost_estimate=pl.CostEstimate(flops=2**28, bytes_accessed=2**22, transcendentals=0),
        name="place",
    )(put, cover, hidden, *messages)


def exchange(arrays, core_first):
    count = len(arrays)
    return [
        array if step == (0, 0) else lax.ppermute(array, "frame", [(i, i ^ step[i % 2]) for i in range(count)])
        for array, step in zip(arrays, steps_of(count, core_first))
    ]


def on_device(grid, conv_weight, conv_bias, depth_kernel, point_weight, occupied, counts):
    channels, frames, height, columns = grid.shape
    tiles, parts = lax.axis_size("tile"), lax.axis_size("frame")
    slots = occupied.shape[1] // parts
    band = bands(conv_weight, height)
    first, second = edge_columns(grid, band)
    first = lax.ppermute(first, "tile", swaps(tiles, 0))
    second = lax.ppermute(second, "tile", swaps(tiles, 1))
    inside = inner(grid, band, conv_bias, occupied, parts)
    hidden, *messages = finish(grid, band, *inside, first, second, parts)
    depth, mix = tables(depth_kernel, point_weight, slots, messages[0])
    updated = temporal(exchange(messages, False), depth, mix)
    put, cover = plan(occupied, counts, GROUP * height, columns // LANES, parts, updated[0])
    return place(hidden, exchange(updated, True), put, cover)


def solution(mesh):
    placed = (P(None, "frame", None, "tile"), P(), P(), P(), P(), P("tile", None), P("tile"))
    return jax.shard_map(
        on_device,
        mesh=mesh,
        in_specs=placed,
        out_specs=P(None, "frame", None, "tile"),
        check_vma=False,
    )
```

```python
import functools

import jax
import jax.numpy as jnp
from jax import lax
from jax.experimental import pallas as pl
from jax.experimental.pallas import tpu as pltpu
from jax.sharding import PartitionSpec as P

GROUP = 8
LANES = 128
MIB = 2**20


def params(mib):
    return pltpu.CompilerParams(vmem_limit_bytes=mib * MIB)


def whole(shape):
    return pl.BlockSpec(shape, lambda *_: (0,) * len(shape))


def dot(a, b, dims=((1,), (0,))):
    return lax.dot_general(a, b, (dims, ((), ())), preferred_element_type=jnp.float32)


def quotient(value, size):
    return value >> (size.bit_length() - 1) if size & (size - 1) == 0 else value // size


def remainder(value, size):
    return value & (size - 1) if size & (size - 1) == 0 else value % size


def iota(shape, dim):
    return lax.broadcasted_iota(jnp.int32, shape, dim)


def edges_kernel(grid_ref, _, first_ref, second_ref, found):
    channels, frames, height, columns = grid_ref.shape
    groups, wide = channels // GROUP, GROUP * height
    count = groups * frames
    even = lax.axis_index("tile") % 2 == 0
    ahead, behind = jnp.where(even, columns - 1, 0), jnp.where(even, 0, columns - 1)
    rows, lanes = iota((16, columns), 0), iota((16, columns), 1)
    pick = (((rows == 0) & (lanes == ahead)) | ((rows == 1) & (lanes == behind))).astype(jnp.bfloat16)
    for g in range(groups):
        for f in range(frames):
            at = g * frames + f
            cells = grid_ref[g * GROUP : (g + 1) * GROUP, f].reshape(wide, columns)
            both = dot(pick, cells, ((1,), (1,)))
            found[at : at + 1, :] = both[0:1]
            found[count + at : count + at + 1, :] = both[1:2]
    first_ref[...] = found[:count].astype(jnp.bfloat16)
    second_ref[...] = found[count:].astype(jnp.bfloat16)


def swaps(count, start):
    partner = {i: i for i in range(count)}
    for i in range(start, count - 1, 2):
        partner[i], partner[i + 1] = i + 1, i
    return sorted(partner.items())


def edge_columns(grid, after):
    channels, frames, height, _ = grid.shape
    shape = jax.ShapeDtypeStruct((channels // GROUP * frames, GROUP * height), jnp.bfloat16)
    return pl.pallas_call(
        edges_kernel,
        in_specs=[pl.BlockSpec(memory_space=pltpu.VMEM), pl.BlockSpec(memory_space=pl.ANY)],
        out_shape=(shape, shape),
        scratch_shapes=[pltpu.VMEM((2 * shape.shape[0], shape.shape[1]), jnp.float32)],
        compiler_params=params(8),
        cost_estimate=pl.CostEstimate(flops=2**28, bytes_accessed=2**21, transcendentals=0),
        name="edge_columns",
    )(grid, after)


def bands_kernel(height, taps_ref, band_ref, spread):
    _, inner, channels = taps_ref.shape
    wide = GROUP * height
    repeat = (iota((inner, wide), 0) == iota((inner, wide), 1) // height).astype(jnp.bfloat16)
    for tap in range(9):
        half = (taps_ref[tap].astype(jnp.float32) * 0.5).astype(jnp.bfloat16)
        spread[tap] = dot(half, repeat, ((0,), (0,)))
    strip = 16
    offset = remainder(iota((height, wide), 1), height) - iota((height, wide), 0)
    offset = offset.astype(jnp.float32).astype(jnp.bfloat16)
    masks = [
        [offset[top : top + strip] == jnp.bfloat16(row - 1) for row in range(3)] for top in range(0, height, strip)
    ]
    for c in range(channels):
        for col in range(3):
            rows = [
                jnp.broadcast_to(spread[3 * row + col, c : c + 1, :], (strip, wide)).astype(jnp.bfloat16)
                for row in range(3)
            ]
            for at, mask in enumerate(masks):
                value = jnp.zeros((strip, wide), jnp.bfloat16)
                for row in range(3):
                    value = jnp.where(mask[row], rows[row], value)
                top = c % GROUP * height + at * strip
                band_ref[c // GROUP, top : top + strip, col * wide : (col + 1) * wide] = value


def bands(conv_weight, height):
    taps = jnp.transpose(conv_weight, (0, 2, 1))
    channels = taps.shape[2]
    groups, wide = channels // GROUP, GROUP * height
    return pl.pallas_call(
        functools.partial(bands_kernel, height),
        out_shape=jax.ShapeDtypeStruct((groups, wide, 3 * wide), jnp.bfloat16),
        scratch_shapes=[pltpu.VMEM((9, channels, wide), jnp.float32)],
        compiler_params=params(8),
        cost_estimate=pl.CostEstimate(flops=2**28, bytes_accessed=2**23, transcendentals=0),
        name="bands",
    )(taps)


def inner_kernel(occupied_ref, bias_ref, grid_ref, band_ref, summed_ref, cells_ref, pick_ref, side_ref):
    channels, frames, height, columns = grid_ref.shape
    halves = columns // LANES
    wide = GROUP * height
    me, count = lax.axis_index("frame"), lax.axis_size("frame")
    slots = occupied_ref.shape[1] // count
    part = GROUP * slots
    rows, lanes = iota((part, wide), 0), iota((part, wide), 1)
    at_slot, at_side = remainder(rows, slots), remainder(iota((part, LANES), 0), slots)
    same_channel, at_row = quotient(lanes, height) == quotient(rows, slots), remainder(lanes, height)
    for d, step in enumerate(steps_of(count)):
        row, side = jnp.zeros((part, wide), jnp.int32), jnp.zeros((part, LANES), jnp.int32)
        first = sent_to(me, step) * slots
        for j in range(slots):
            block = occupied_ref[0, first + j]
            row = jnp.where(at_slot == j, quotient(block, halves), row)
            side = jnp.where(at_side == j, remainder(block, halves), side)
        pick_ref[d * part : (d + 1) * part, :] = (same_channel & (at_row == row)).astype(jnp.bfloat16)
        side_ref[d * part : (d + 1) * part, :] = side

    tile_lanes = iota((wide, LANES), 1)
    is_first, is_last = tile_lanes == 0, tile_lanes == LANES - 1
    nothing = jnp.zeros((wide, LANES), jnp.bfloat16)

    def shifted(g, f):
        cells = grid_ref[g * GROUP : (g + 1) * GROUP, f].reshape(wide, columns)
        tiles = [cells[:, side * LANES : (side + 1) * LANES] for side in range(halves)]
        right = [pltpu.roll(tile, 1, 1) for tile in tiles]
        left = [pltpu.roll(tile, LANES - 1, 1) for tile in tiles]
        before = [jnp.where(is_first, *pair) for pair in zip([nothing] + right[:-1], right)]
        after = [jnp.where(is_last, *pair) for pair in zip(left[1:] + [nothing], left)]
        return jnp.concatenate([jnp.concatenate(before, axis=1), cells, jnp.concatenate(after, axis=1)], axis=0)

    items = [(g, f) for g in range(channels // GROUP) for f in range(frames)]
    ready = shifted(*items[0])
    for (g, f), following in zip(items, items[1:] + [None]):
        summed = dot(band_ref[g], ready)
        if following is not None:
            ready = shifted(*following)
        for out in range(GROUP):
            inside = slice(out * height, (out + 1) * height)
            summed_ref[g, f, inside, :] = summed[inside] + 0.5 * bias_ref[g * GROUP + out]
            cells_ref[g, f, inside, :] = grid_ref[g * GROUP + out, f].astype(jnp.float32)


def inner(grid, band, conv_bias, occupied, parts):
    channels, frames, height, columns = grid.shape
    part = GROUP * (occupied.shape[1] // parts)
    smem, vmem = pl.BlockSpec(memory_space=pltpu.SMEM), pl.BlockSpec(memory_space=pltpu.VMEM)
    wide = jax.ShapeDtypeStruct((channels // GROUP, frames, GROUP * height, columns), jnp.float32)
    return pl.pallas_call(
        inner_kernel,
        in_specs=[smem, smem, vmem, vmem],
        out_shape=(
            wide,
            wide,
            jax.ShapeDtypeStruct((parts * part, GROUP * height), jnp.bfloat16),
            jax.ShapeDtypeStruct((parts * part, LANES), jnp.int32),
        ),
        compiler_params=params(8),
        cost_estimate=pl.CostEstimate(flops=2**31, bytes_accessed=2**23, transcendentals=0),
        name="inner",
    )(occupied, conv_bias, grid, band)


def steps_of(count, core_first=False):
    mixed = [(4, 2), (2, 4), (5, 3), (3, 5)] if count >= 8 else []
    seen = {0, 1} | {a for a, _ in mixed}
    across = mixed + [(d, d) for d in range(count) if d not in seen]
    return [(0, 0), (1, 1)] + across if core_first else [(0, 0)] + across + [(1, 1)]


def sent_to(me, step):
    return me ^ jnp.where(remainder(me, 2) == 0, step[0], step[1])


def got_from(me, step):
    return sent_to(me, step) if step[0] % 2 == 0 else sent_to(me, step[::-1])


def finish_kernel(band_ref, summed_ref, cells_ref, pick_ref, side_ref, first_ref, second_ref, hidden_ref, *message_refs):
    channels, frames, height, columns = hidden_ref.shape
    halves = columns // LANES
    wide = GROUP * height
    part = pick_ref.shape[0] // len(message_refs)
    tile, tiles = lax.axis_index("tile"), lax.axis_size("tile")
    even = tile % 2 == 0
    first, second = first_ref[...].astype(jnp.float32), second_ref[...].astype(jnp.float32)
    left = jnp.where(tile > 0, jnp.where(even, second, first), 0.0)
    right = jnp.where(tile < tiles - 1, jnp.where(even, first, second), 0.0)
    rim = 16
    rim_rows = iota((rim, wide), 0)
    blank = jnp.zeros((LANES - rim, wide), jnp.bfloat16)

    def edge_terms(g):
        before, after = [], []
        for f in range(frames):
            at = slice(g * frames + f, g * frames + f + 1)
            before += [jnp.where(rim_rows == 0, left[at], 0.0).astype(jnp.bfloat16), blank]
            after += [blank, jnp.where(rim_rows == rim - 1, right[at], 0.0).astype(jnp.bfloat16)]
        return (
            dot(band_ref[g, :, :wide], jnp.concatenate(before, axis=0), ((1,), (1,))),
            dot(band_ref[g, :, 2 * wide :], jnp.concatenate(after, axis=0), ((1,), (1,))),
        )

    def activate(g, at_left, at_right):
        for f in range(frames):
            across = slice(f * LANES, (f + 1) * LANES)
            for out in range(GROUP):
                c = g * GROUP + out
                part = slice(out * height, (out + 1) * height)
                half = summed_ref[g, f, part, :]
                tiles = [half[:, side * LANES : (side + 1) * LANES] for side in range(halves)]
                tiles[0] += at_left[part, across]
                tiles[-1] += at_right[part, across]
                half = jnp.concatenate(tiles, axis=1)
                hidden = cells_ref[g, f, part, :] + (half + half * jnp.tanh(half))
                hidden_ref[c, f] = hidden.astype(jnp.bfloat16)

    def pick(g):
        return [
            dot(pick_ref[...], hidden_ref[g * GROUP : (g + 1) * GROUP, f].reshape(wide, columns))
            for f in range(frames)
        ]

    def send(g, picks):
        for f, picked in enumerate(picks):
            chosen = picked[:, :LANES]
            for side in range(1, halves):
                chosen = jnp.where(side_ref[...] == side, picked[:, side * LANES : (side + 1) * LANES], chosen)
            chosen = chosen.astype(jnp.bfloat16)
            for d, message_ref in enumerate(message_refs):
                message_ref[f, g * part : (g + 1) * part, :] = chosen[d * part : (d + 1) * part]

    groups = channels // GROUP
    terms = edge_terms(0)
    for g in range(groups):
        current = terms
        picks = pick(g - 1) if g > 0 else None
        terms = edge_terms(g + 1) if g + 1 < groups else None
        activate(g, *current)
        if picks is not None:
            send(g - 1, picks)
    send(groups - 1, pick(groups - 1))


def finish(grid, band, summed, cells, pick, side, first, second, parts):
    channels, frames, _, _ = grid.shape
    slots = pick.shape[0] // (GROUP * parts)
    vmem = pl.BlockSpec(memory_space=pltpu.VMEM)
    return pl.pallas_call(
        finish_kernel,
        in_specs=[vmem] * 7,
        out_shape=[jax.ShapeDtypeStruct(grid.shape, jnp.bfloat16)]
        + [jax.ShapeDtypeStruct((frames, channels * slots, LANES), jnp.bfloat16)] * parts,
        compiler_params=params(8),
        cost_estimate=pl.CostEstimate(flops=2**30, bytes_accessed=2**23, transcendentals=2**20),
        name="finish",
    )(band, summed, cells, pick, side, first, second)


def tables_kernel(depth_ref, point_ref, _, table_ref, mix_ref):
    layers, channels, _ = point_ref.shape
    taps = depth_ref.shape[0]
    tall = mix_ref.shape[1]
    slots = tall // channels
    same_channel = iota((tall, channels), 0) // slots == iota((tall, channels), 1)
    up = same_channel.astype(jnp.bfloat16)
    across = (iota((channels, tall), 1) // slots == iota((channels, tall), 0)).astype(jnp.bfloat16)
    same_slot = iota((tall, tall), 0) % slots == iota((tall, tall), 1) % slots
    for layer in range(layers):
        for tap in range(taps):
            row = 0.5 * depth_ref[tap, layer : layer + 1, :]
            column = jnp.sum(jnp.where(same_channel, row, 0.0), axis=1, keepdims=True)
            table_ref[layer * taps + tap] = jnp.broadcast_to(column, table_ref.shape[1:])
        spread = dot(dot(up, point_ref[layer]).astype(jnp.bfloat16), across)
        mix_ref[layer] = jnp.where(same_slot, spread, 0.0).astype(jnp.bfloat16)


def tables(depth_kernel, point_weight, slots, after):
    layers, taps, channels = depth_kernel.shape
    vmem = pl.BlockSpec(memory_space=pltpu.VMEM)
    return pl.pallas_call(
        tables_kernel,
        in_specs=[vmem, vmem, pl.BlockSpec(memory_space=pl.ANY)],
        out_shape=(
            jax.ShapeDtypeStruct((layers * taps, channels * slots, LANES), jnp.float32),
            jax.ShapeDtypeStruct((layers, channels * slots, channels * slots), jnp.bfloat16),
        ),
        compiler_params=params(8),
        cost_estimate=pl.CostEstimate(flops=2**27, bytes_accessed=2**22, transcendentals=0),
        name="tables",
    )(jnp.transpose(depth_kernel, (1, 0, 2)), point_weight, after)


def temporal_kernel(sources, depth_ref, mix_ref, *refs):
    message_refs, out_refs = refs[:sources], refs[sources : 2 * sources]
    state, squashed, final = refs[2 * sources :]
    me = lax.axis_index("frame")
    local, tall, lanes = message_refs[0].shape
    frames = sources * local
    layers = mix_ref.shape[0]
    taps = depth_ref.shape[0] // layers
    quads, _, width = squashed.shape
    quad = width // lanes
    for step, message_ref in zip(steps_of(sources), message_refs):
        for f in range(local):
            state[got_from(me, step) * local + f] = message_ref[f].astype(jnp.float32)
    height = 16

    def blend(layer, q):
        spacing = 2**layer
        inside = range(q * quad, (q + 1) * quad)
        for top in range(0, tall, height):
            part = slice(top, top + height)
            scale = [depth_ref[layer * taps + tap, part] for tap in range(taps)]
            needed = {f - tap * spacing for f in inside for tap in range(taps)}
            series = {f: state[f, part] for f in sorted(needed) if f >= 0}
            for f in inside:
                half = scale[0] * series[f]
                for tap in range(1, taps):
                    if f >= tap * spacing:
                        half += scale[tap] * series[f - tap * spacing]
                across = slice((f - q * quad) * lanes, (f - q * quad + 1) * lanes)
                squashed[q, part, across] = (half + half * jnp.tanh(half)).astype(jnp.bfloat16)

    def update(layer, q, mixed):
        for f in range(q * quad, (q + 1) * quad):
            after = state[f] + mixed[:, (f - q * quad) * lanes : (f - q * quad + 1) * lanes]
            if layer + 1 < layers:
                state[f] = after
            else:
                final[f] = after.astype(jnp.bfloat16)

    waiting = None
    for layer in range(layers):
        for q in reversed(range(quads)):
            reads = {(f - tap * 2**layer) // quad for f in range(q * quad, (q + 1) * quad) for tap in range(taps)}
            late = waiting is not None and waiting[1] not in reads
            if waiting is not None and not late:
                update(*waiting)
            blend(layer, q)
            if late:
                update(*waiting)
            waiting = layer, q, dot(mix_ref[layer], squashed[q])
    update(*waiting)
    for step, out_ref in zip(steps_of(sources, True), out_refs):
        for f in range(local):
            out_ref[f] = final[sent_to(me, step) * local + f]


def temporal(messages, depth, mix):
    sources = len(messages)
    local, tall, lanes = messages[0].shape
    vmem = pl.BlockSpec(memory_space=pltpu.VMEM)
    return pl.pallas_call(
        functools.partial(temporal_kernel, sources),
        in_specs=[vmem, vmem] + [vmem] * sources,
        out_shape=[jax.ShapeDtypeStruct(messages[0].shape, jnp.bfloat16)] * sources,
        scratch_shapes=[
            pltpu.VMEM((sources * local, tall, lanes), jnp.float32),
            pltpu.VMEM((sources * local // 4, tall, 4 * lanes), jnp.bfloat16),
            pltpu.VMEM((sources * local, tall, lanes), jnp.bfloat16),
        ],
        compiler_params=params(12),
        cost_estimate=pl.CostEstimate(flops=2**30, bytes_accessed=2**21, transcendentals=2**21),
        name="temporal",
    )(depth, mix, *messages)


def plan_kernel(sources, occupied_ref, counts_ref, _, put_ref, cover_ref):
    me = lax.axis_index("frame")
    halves, wide, tall = put_ref.shape
    part = tall // sources
    slots = part // GROUP
    height = wide // GROUP
    rows, lanes = iota((part, wide), 0), iota((part, wide), 1)
    same_channel, at_slot, at_row = lanes // height == rows // slots, rows % slots, lanes % height
    for side in range(halves):
        hits = []
        for step in steps_of(sources, True):
            row = jnp.full((part, wide), -1, jnp.int32)
            for j in range(slots):
                slot = got_from(me, step) * slots + j
                block = occupied_ref[0, slot]
                used = (slot < counts_ref[0]) & (block % halves == side)
                row = jnp.where(at_slot == j, jnp.where(used, block // halves, -1), row)
            hits.append((same_channel & (at_row == row)).astype(jnp.float32))
        put = jnp.transpose(jnp.concatenate(hits, axis=0)).astype(jnp.bfloat16)
        put_ref[side] = put
        cover_ref[side] = dot(put, jnp.ones((tall, LANES), jnp.bfloat16))


def plan(occupied, counts, wide, halves, sources, after):
    smem = pl.BlockSpec(memory_space=pltpu.SMEM)
    return pl.pallas_call(
        functools.partial(plan_kernel, sources),
        in_specs=[smem, smem, pl.BlockSpec(memory_space=pl.ANY)],
        out_shape=(
            jax.ShapeDtypeStruct((halves, wide, GROUP * occupied.shape[1]), jnp.bfloat16),
            jax.ShapeDtypeStruct((halves, wide, LANES), jnp.float32),
        ),
        compiler_params=params(8),
        cost_estimate=pl.CostEstimate(flops=2**27, bytes_accessed=2**22, transcendentals=0),
        name="plan",
    )(occupied, counts, after)


def place_kernel(sources, put_ref, cover_ref, hidden_ref, *refs):
    message_refs, (out_hbm, out_ref, sems) = refs[:sources], refs[sources:]
    channels, frames, height, columns = hidden_ref.shape
    halves = columns // LANES
    wide = GROUP * height
    part = put_ref.shape[2] // sources

    def group_copy(g):
        cells = pl.ds(g * GROUP, GROUP)
        return pltpu.make_async_copy(out_ref.at[cells], out_hbm.at[cells], sems.at[g])

    def spread(g):
        rows = slice(g * part, (g + 1) * part)
        updated = jnp.concatenate(
            [jnp.concatenate([ref[f, rows, :] for f in range(frames)], axis=1) for ref in message_refs], axis=0
        )
        return [dot(put_ref[side], updated) for side in range(halves)]

    def merge(g, spreads):
        base = g * GROUP
        for side in range(halves):
            across = slice(side * LANES, (side + 1) * LANES)
            for f in range(frames):
                cells = hidden_ref[base : base + GROUP, f, :, across].reshape(wide, LANES).astype(jnp.float32)
                merged = jnp.where(cover_ref[side] > 0.5, spreads[side][:, f * LANES : (f + 1) * LANES], cells)
                out_ref[base : base + GROUP, f, :, across] = merged.astype(jnp.bfloat16).reshape(GROUP, height, LANES)
        group_copy(g).start()

    groups = channels // GROUP
    following = spread(0)
    for g in range(groups):
        current = following
        following = spread(g + 1) if g + 1 < groups else None
        merge(g, current)
    for g in range(groups):
        group_copy(g).wait()


def place(hidden, messages, put, cover):
    channels = hidden.shape[0]
    sources = len(messages)
    vmem, anywhere = pl.BlockSpec(memory_space=pltpu.VMEM), pl.BlockSpec(memory_space=pl.ANY)
    return pl.pallas_call(
        functools.partial(place_kernel, sources),
        in_specs=[vmem, vmem, vmem] + [vmem] * sources,
        out_specs=anywhere,
        out_shape=jax.ShapeDtypeStruct(hidden.shape, jnp.bfloat16),
        scratch_shapes=[
            pltpu.VMEM(hidden.shape, jnp.bfloat16),
            pltpu.SemaphoreType.DMA((channels // GROUP,)),
        ],
        compiler_params=params(8),
        cost_estimate=pl.CostEstimate(flops=2**28, bytes_accessed=2**22, transcendentals=0),
        name="place",
    )(put, cover, hidden, *messages)


def exchange(arrays, core_first):
    count = len(arrays)
    return [
        array if step == (0, 0) else lax.ppermute(array, "frame", [(i, i ^ step[i % 2]) for i in range(count)])
        for array, step in zip(arrays, steps_of(count, core_first))
    ]


def on_device(grid, conv_weight, conv_bias, depth_kernel, point_weight, occupied, counts):
    channels, frames, height, columns = grid.shape
    tiles, parts = lax.axis_size("tile"), lax.axis_size("frame")
    slots = occupied.shape[1] // parts
    band = bands(conv_weight, height)
    first, second = edge_columns(grid, band)
    first = lax.ppermute(first, "tile", swaps(tiles, 0))
    second = lax.ppermute(second, "tile", swaps(tiles, 1))
    inside = inner(grid, band, conv_bias, occupied, parts)
    hidden, *messages = finish(grid, band, *inside, first, second, parts)
    depth, mix = tables(depth_kernel, point_weight, slots, messages[0])
    updated = temporal(exchange(messages, False), depth, mix)
    put, cover = plan(occupied, counts, GROUP * height, columns // LANES, parts, updated[0])
    return place(hidden, exchange(updated, True), put, cover)


def solution(mesh):
    placed = (P(None, "frame", None, "tile"), P(), P(), P(), P(), P("tile", None), P("tile"))
    return jax.shard_map(
        on_device,
        mesh=mesh,
        in_specs=placed,
        out_specs=P(None, "frame", None, "tile"),
        check_vma=False,
    )
```
